256 devices in a mesh: bin: 8 (over z_hi, x), slab: 32 (over z_lo, y, core).
Axes of the slice: x: 4, y: 4, z: 8 (z_hi: 2, z_lo: 4; z = z_hi * 4 + z_lo), core: 2. Of those that a mesh axis runs over, the one named last changes fastest.
Arguments:
- sample_data: bfloat16 [8192, 2048], P(('bin', 'slab')), may hold values from -6 to 6
- block_route: int32 [8192, 1], P(('bin', 'slab')), may hold values from 0 to 23, as said below
- spoke_index: int32 [8192], P(('bin', 'slab')), may hold values from 0 to 32767
- segment_index: int32 [8192], P(('bin', 'slab')), may hold values from 0 to 11
- sample_count: int32 [8192], P(('bin', 'slab')), may hold values from 16 to 32
- sensitivity: bfloat16 [96, 262144], P(None, 'slab'), may hold values from -6 to 6
- image: float32 [8, 96, 8192], P('bin', None, 'slab'), may hold values from -6 to 6
- tv_weight: float32 [8, 96, 4096], P('bin', None, 'slab'), may hold values from 0.3 to 3
Outputs:
- gradient: float32 [8, 96, 8192], P('bin', None, 'slab')
The draws below stay inside these ranges and needn't reach their ends.
Inputs may be any that keep to these rules, and one draw needn't show every extreme that they name: `block_route`: among the 32 blocks of one device no value occurs more than 4 times; for every slab index one value occurs exactly 4 times on every device with that slab index.
All inputs are finite; a program needn't handle non-finite values.
Results may differ from the reference program's by a relative error of at most 0.0037.
Values may be sent and summed in bfloat16 or wider, within the bound.
A program may use at most 128 MiB of HBM per device.

```python
import math
import jax
import jax.numpy as jnp
from jax import lax

C = 32
NG = 384
NXI = 256
WY = 16
RO = 384
P_SIZE = 32
R = 40
KP = 3
BLKB = 4
CAPK = 4
NBLK = 32
BLOCKS = 8192
KZ = 96
N_BIN = 8
N_SLAB = 32


def draw_block_route(key, part):
    key = jax.random.fold_in(key, 7)
    device_count = N_BIN * N_SLAB
    key_count = N_BIN * KP
    candidates = key_count * CAPK
    bin_key, hot_key, score_key, order_key = jax.random.split(key, 4)
    bin_weight = jnp.left_shift(jnp.int32(1), jax.random.randint(bin_key, (N_BIN,), 0, 4))
    hot_route = jax.random.randint(hot_key, (N_SLAB,), 0, key_count)
    cand_route = jnp.arange(candidates, dtype=jnp.int32) // CAPK
    cand_weight = bin_weight[cand_route // KP]
    raw_score = jax.random.randint(score_key, (device_count, candidates), 0, 1024)
    scored = raw_score * cand_weight[None, :]
    device_hot = jnp.tile(hot_route, N_BIN)
    scored = jnp.where(cand_route[None, :] == device_hot[:, None], 8192, scored)
    ranked = scored * candidates + jnp.arange(candidates, dtype=jnp.int32)[None, :]
    top_values, chosen = lax.top_k(ranked, NBLK)
    picked = cand_route[chosen]
    order_keys = jax.random.split(order_key, device_count)
    shuffled = jax.vmap(jax.random.permutation)(order_keys, picked)
    return shuffled.reshape(device_count * NBLK, 1).astype(jnp.int32)


def set_ends(drawn, rng, low, top_value):
    place = [jax.random.randint(jax.random.fold_in(rng, axis), (), 0, length) for axis, length in enumerate(drawn.shape)]
    longest = drawn.shape.index(max(drawn.shape))
    neighbour = place[:longest] + [(place[longest] + 1) % drawn.shape[longest]] + place[longest + 1:]
    return drawn.at[tuple(place)].set(low).at[tuple(neighbour)].set(top_value)


def shard_levels(own_key, shape, cuts, least, top_value):
    loudness = 1.0
    for axis_at, blocks in cuts:
        heights = jax.random.uniform(jax.random.fold_in(jax.random.fold_in(own_key, 6), axis_at), (blocks,), jnp.float32, least / len(cuts), top_value / len(cuts))
        loudness = loudness * jnp.repeat(jnp.exp(heights), shape[axis_at] // blocks).reshape((-1,) + (1,) * (len(shape) - 1 - axis_at))
    return loudness


def noise(stream_key, extent, width, most, cuts=(), held_as=jnp.bfloat16):
    drawn = jax.random.normal(stream_key, extent, jnp.float32) * width
    if len(cuts) > 0:
        drawn = shard_levels(stream_key, extent, cuts, -0.22, 0.18) * drawn
    return jnp.clip(drawn, min=-most, max=most).astype(held_as)


def setup_inputs(seed: int = 0) -> dict:
    arg_keys = jax.random.split(jax.random.key(seed), 9)
    return {
        "sample_data": noise(arg_keys[0], (BLOCKS, P_SIZE * 2 * C), 1.0, 6.0, ((0, 256),)),
        "block_route": draw_block_route(jax.random.fold_in(arg_keys[8], 71), 0),
        "spoke_index": set_ends(jax.random.randint(arg_keys[2], (BLOCKS,), 0, 32768), jax.random.fold_in(arg_keys[2], 1), 0, 32767).astype(jnp.int32),
        "segment_index": set_ends(jax.random.randint(arg_keys[3], (BLOCKS,), 0, RO // P_SIZE), jax.random.fold_in(arg_keys[3], 1), 0, (RO // P_SIZE) - 1).astype(jnp.int32),
        "sample_count": set_ends(jax.random.randint(arg_keys[4], (BLOCKS,), P_SIZE // 2, P_SIZE + 1), jax.random.fold_in(arg_keys[4], 1), P_SIZE // 2, P_SIZE).astype(jnp.int32),
        "sensitivity": noise(arg_keys[5], (KZ, NXI * 2 * C * WY), 1.0, 6.0, ((1, 32),)),
        "image": noise(arg_keys[6], (N_BIN, KZ, NXI * 2 * WY), 1.0, 6.0, ((0, 8), (2, 32)), jnp.float32),
        "tv_weight": jnp.clip(jnp.exp(math.log(3.0) - 2.3025851 * jax.random.uniform(arg_keys[7], (N_BIN, KZ, NXI * WY), jnp.float32) ** shard_levels(arg_keys[7], (N_BIN, KZ, NXI * WY), ((0, 8), (2, 32)), -0.2, 0.2)), 0.3, 3.0),
    }


SMOOTHING = 0.5
GOLDEN_STEP = 40503
TURN_STEPS = 65536

def spline_weight(offset):
    distance = jnp.abs(offset)
    inside = 2.0 / 3.0 - distance * distance + 0.5 * distance * distance * distance
    outside = jnp.maximum(2.0 - distance, 0.0) ** 3 / 6.0
    return jnp.where(distance < 1.0, inside, outside)

def phase_table(out_index, input_index, modulus):
    turn_index = out_index[:, None] * input_index[None, :] % modulus
    angles = 2.0 * math.pi / modulus * turn_index.astype(jnp.float32)
    return jnp.concatenate([jnp.cos(angles), jnp.sin(angles)], axis=0).astype(jnp.bfloat16)

def sample_coords(spoke_ids, segment, samples, readout, grid):
    fraction = (spoke_ids * GOLDEN_STEP % TURN_STEPS).astype(jnp.float32) / TURN_STEPS
    angles = 2.0 * math.pi * fraction
    sample_step = jnp.arange(samples, dtype=jnp.int32)
    radial = ((segment[:, None] * samples + sample_step[None, :] - readout // 2).astype(jnp.float32) + 0.5) * ((grid - 8) / readout)
    coord_x = grid / 2 + radial * jnp.cos(angles)[:, None]
    coord_y = grid / 2 + radial * jnp.sin(angles)[:, None]
    return (coord_x, coord_y)

def tile_lines(data, spoke_ids, segment, counts, samples, readout, grid, tile, rows, coils):
    tile_count = data.shape[0]
    coord_x, coord_y = sample_coords(spoke_ids, segment, samples, readout, grid)
    sample_step = jnp.arange(samples, dtype=jnp.int32)
    usable = (sample_step[None, :] < counts[:, None]).astype(jnp.float32)
    tile_start = (jnp.floor(lax.optimization_barrier(jnp.min(coord_x, axis=1))) - 2.0).astype(jnp.int32)
    columns = tile_start[:, None] + jnp.arange(tile, dtype=jnp.int32)[None, :]
    across_bins = spline_weight(coord_x[:, :, None] - columns[:, None, :].astype(jnp.float32)) * usable[:, :, None]
    tap_cells = (jnp.floor(coord_y).astype(jnp.int32) - 1)[:, :, None] + jnp.arange(4, dtype=jnp.int32)[None, None, :]
    tap_weight = spline_weight(coord_y[:, :, None] - tap_cells.astype(jnp.float32))
    row_start_offsets = jnp.arange(rows, dtype=jnp.int32) - rows // 2
    turn_index = row_start_offsets[None, None, None, :] * (tap_cells[:, :, :, None] - grid // 2) % grid
    angles = 2.0 * math.pi / grid * turn_index.astype(jnp.float32)
    real_weight = lax.optimization_barrier(jnp.sum(tap_weight[:, :, :, None] * jnp.cos(angles), axis=2))
    imag_weight = lax.optimization_barrier(jnp.sum(tap_weight[:, :, :, None] * jnp.sin(angles), axis=2))
    values = data.astype(jnp.float32).reshape(tile_count, samples, 2, coils)
    data_real = values[:, :, 0, :, None]
    data_imag = values[:, :, 1, :, None]
    real_part = real_weight[:, :, None, :] * data_real - imag_weight[:, :, None, :] * data_imag
    imag_part = real_weight[:, :, None, :] * data_imag + imag_weight[:, :, None, :] * data_real
    weighted_values = jnp.stack([real_part, imag_part], axis=2).astype(jnp.bfloat16)
    weighted_values = weighted_values.reshape(tile_count, samples, 2 * coils * rows)
    return (across_bins.astype(jnp.bfloat16), weighted_values, columns % grid)

def combine_coils(transformed, maps, columns, coils, rows):
    kz_depth = maps.shape[0]
    halves = transformed.reshape(2, kz_depth, columns, 2, coils, rows)
    sens_values = maps.astype(jnp.float32).reshape(kz_depth, columns, 2, coils, rows)
    image_real = halves[0, :, :, 0] - halves[1, :, :, 1]
    image_imag = halves[0, :, :, 1] + halves[1, :, :, 0]
    sens_real = sens_values[:, :, 0]
    sens_imag = sens_values[:, :, 1]
    out_real = lax.optimization_barrier(jnp.sum(sens_real * image_real + sens_imag * image_imag, axis=2))
    out_imag = lax.optimization_barrier(jnp.sum(sens_real * image_imag - sens_imag * image_real, axis=2))
    return jnp.stack([out_real, out_imag], axis=2)

def edge_flux(lower_image, upper_image, weight):
    difference = upper_image - lower_image
    magnitude = jnp.sqrt(lax.optimization_barrier(jnp.sum(difference * difference, axis=-2)) + SMOOTHING * SMOOTHING)
    return weight[..., None, :] * difference / magnitude[..., None, :]

def reference(sample_data, block_route, spoke_index, segment_index, sample_count, sensitivity, image, tv_weight):
    features = 2 * C * WY
    columns_dev = NXI // N_SLAB

    def by_column(values):
        return values.reshape((N_BIN, N_SLAB, NBLK) + values.shape[1:])
    data_cols = by_column(sample_data)
    route_cols = by_column(block_route[:, 0])
    spoke_cols = by_column(spoke_index)
    segment_cols = by_column(segment_index)
    count_cols = by_column(sample_count)
    x_table = phase_table(jnp.arange(NXI, dtype=jnp.int32) - NXI // 2, jnp.arange(NG, dtype=jnp.int32) - NG // 2, NG)
    x_table = lax.optimization_barrier(x_table).astype(jnp.float32)

    def grid_column(column):

        def pick(values):
            chosen = lax.dynamic_index_in_dim(values, column, 1, keepdims=False)
            return chosen.reshape((N_BIN * NBLK,) + values.shape[3:])
        across_bins, weighted_values, columns = tile_lines(pick(data_cols), pick(spoke_cols), pick(segment_cols), pick(count_cols), P_SIZE, RO, NG, R, WY, C)
        across_bins, weighted_values = lax.optimization_barrier((across_bins, weighted_values))
        tile_partial_sums = jnp.einsum('sbm,sbg->smg', across_bins.astype(jnp.float32), weighted_values.astype(jnp.float32))
        targets = pick(route_cols)[:, None] * NG + columns
        gridded = jax.ops.segment_sum(tile_partial_sums.reshape(-1, features), targets.reshape(-1), num_segments=N_BIN * KP * NG)
        gridded = lax.optimization_barrier(gridded.astype(jnp.bfloat16)).astype(jnp.float32)
        transformed = jnp.einsum('xk,nkf->nxf', x_table, gridded.reshape(N_BIN * KP, NG, features))
        transformed = transformed.reshape(N_BIN * KP, 2, NXI, 2, C * WY)
        real_part = transformed[:, 0, :, 0] - transformed[:, 1, :, 1]
        imag_part = transformed[:, 0, :, 1] + transformed[:, 1, :, 0]
        spectrum = jnp.stack([real_part, imag_part], axis=2).astype(jnp.bfloat16)
        return spectrum.reshape(N_BIN, KP, NXI, features)
    spectra = lax.map(grid_column, jnp.arange(N_SLAB, dtype=jnp.int32))
    z_index = jnp.arange(KZ, dtype=jnp.int32) - KZ // 2
    z_table = lax.optimization_barrier(phase_table(z_index, z_index, KZ)).astype(jnp.float32)
    scaling = 1.0 / math.sqrt(P_SIZE * N_BIN * BLKB * KZ * C / KP)

    def image_block(block_index):
        first = block_index * columns_dev
        piece = lax.dynamic_slice_in_dim(spectra, first, columns_dev, 3)
        piece = jnp.transpose(piece, (1, 0, 2, 3, 4)).reshape(N_BIN, KZ, columns_dev * features).astype(jnp.float32)
        transformed = jnp.einsum('zk,bkm->bzm', z_table, piece)
        maps = lax.dynamic_slice_in_dim(sensitivity, first * features, columns_dev * features, 1)

        def per_bin(single):
            return combine_coils(single, maps, columns_dev, C, WY)
        return jax.vmap(per_bin)(transformed)
    blocks = lax.map(image_block, jnp.arange(N_SLAB, dtype=jnp.int32))
    data_term = jnp.transpose(blocks, (1, 2, 0, 3, 4, 5)).reshape(N_BIN, KZ, NXI, 2, WY) * scaling
    current = image.reshape(N_BIN, KZ, NXI, 2, WY)
    weight = tv_weight.reshape(N_BIN, KZ, NXI, WY)
    edge_terms = edge_flux(current[:-1], current[1:], weight[:-1])
    zeros_row = jnp.zeros_like(edge_terms[:1])
    coupling = jnp.concatenate([zeros_row, edge_terms], axis=0) - jnp.concatenate([edge_terms, zeros_row], axis=0)
    gradient = coupling - data_term
    return gradient.reshape(N_BIN, KZ, NXI * 2 * WY)
```

```python
import functools
import math

import jax
import jax.numpy as jnp
import ml_dtypes
import numpy as np
from jax import lax
from jax.experimental import pallas as pl
from jax.experimental.pallas import tpu as pltpu
from jax.sharding import PartitionSpec as P

C = 32
NG = 384
NXI = 256
WY = 16
RO = 384
P_SIZE = 32
KP = 3
BLKB = 4
CAPK = 4

SMOOTHING = 0.5
GOLDEN_STEP = 40503
TURN_STEPS = 65536

F32 = jnp.float32
BF16 = jnp.bfloat16
LANES = 128
PC = 2 * C
ROUTE_ROWS = KP * PC
COIL_GROUPS = 4
GC = C // COIL_GROUPS
MESH = pl.DeviceIdType.MESH
FAR = -1000.0


def iota(shape, dim):
    return lax.broadcasted_iota(jnp.int32, shape, dim)


def turn_waves(turns):
    quarter = jnp.floor(4.0 * turns + 0.5)
    angle = (2.0 * math.pi) * (turns - 0.25 * quarter)
    sq = angle * angle
    sine = angle + angle * sq * (
        -1.0 / 6 + sq * (1.0 / 120 + sq * (-1.0 / 5040 + sq * (1.0 / 362880)))
    )
    cosine = 1.0 + sq * (
        -0.5 + sq * (1.0 / 24 + sq * (-1.0 / 720 + sq * (1.0 / 40320 + sq * (-1.0 / 3628800))))
    )
    turn = quarter - 4.0 * jnp.floor(0.25 * quarter)
    odd = (turn == 1.0) | (turn == 3.0)
    first = jnp.where(odd, sine, cosine)
    second = jnp.where(odd, cosine, sine)
    cos_out = jnp.where((turn == 1.0) | (turn == 2.0), -first, first)
    sin_out = jnp.where(turn >= 2.0, -second, second)
    return cos_out, sin_out


def spline_weight(offset):
    distance = jnp.abs(offset)
    inside = 2.0 / 3.0 + distance * distance * (0.5 * distance - 1.0)
    rest = jnp.maximum(2.0 - distance, 0.0)
    return jnp.where(distance < 1.0, inside, rest * rest * (rest * (1.0 / 6.0)))


def all_bytes(ref, sem):
    pltpu.make_async_copy(ref, ref, sem).wait()


def route_kernel(
    bins,
    data_ref,
    route_ref,
    spoke_ref,
    segment_ref,
    count_ref,
    image_ref,
    weight_ref,
    tiles_out,
    coords_out,
    above_out,
    below_out,
    below_weight_out,
    stacked,
    placed_rows,
    tiles,
    coords,
    local_sems,
    send_sems,
    recv_sems,
):
    me = lax.axis_index("bin")
    barrier = pltpu.get_barrier_semaphore()
    for step in range(1, bins):
        pl.semaphore_signal(
            barrier, inc=1, device_id={"bin": lax.rem(me + step, bins)}, device_id_type=MESH
        )

    blocks = data_ref.shape[0]
    row = iota((blocks, LANES), 0)
    lane = iota((blocks, LANES), 1)
    lane_block = lane & (blocks - 1)
    route_col = jnp.broadcast_to(route_ref[...].astype(F32), (blocks, LANES))
    route_row = jnp.sum(jnp.where(row == lane_block, route_col, 0.0), axis=0, keepdims=True)
    same = route_col == jnp.broadcast_to(route_row, (blocks, LANES))
    rank_row = jnp.sum(jnp.where(same & (row < lane_block), 1.0, 0.0), axis=0, keepdims=True)
    rank_col = jnp.sum(jnp.where(same & (lane < row), 1.0, 0.0), axis=1, keepdims=True)
    slot_row = route_row * CAPK + rank_row

    def column(ref_row):
        spread = jnp.broadcast_to(ref_row.astype(F32), (blocks, blocks))
        eye = iota((blocks, blocks), 0) == iota((blocks, blocks), 1)
        return jnp.sum(jnp.where(eye, spread, 0.0), axis=1, keepdims=True)

    turn_row = (spoke_ref[...] * GOLDEN_STEP) & (TURN_STEPS - 1)
    columns = [
        column(turn_row >> 8),
        column(turn_row & 255),
        column(segment_ref[...]),
        column(count_ref[...]),
    ]
    slot_hit = rank_col == (lane & (CAPK - 1)).astype(F32)
    picks = [jnp.where(slot_hit, value, 0.0) for value in columns]
    picks = jnp.concatenate(picks, axis=1).astype(BF16)
    picks = jnp.concatenate(
        [picks, jnp.zeros((LANES - blocks, len(columns) * LANES), BF16)], axis=0
    )
    rows = 8 * bins
    out_row = iota((rows, LANES), 0)
    out_lane = iota((rows, LANES), 1)
    part = out_row & 7
    is_x = part < KP
    partition = jnp.where(is_x, part, part - KP)
    row_route = jnp.where(part < 2 * KP, KP * (out_row >> 3) + partition, -1).astype(F32)
    chosen = (row_route == jnp.broadcast_to(route_row, (rows, LANES))) & (out_lane < blocks)
    spread = jnp.dot(
        jnp.where(chosen, 1.0, 0.0).astype(BF16), picks, preferred_element_type=F32
    )
    turns = (256.0 * spread[:, :LANES] + spread[:, LANES : 2 * LANES]) * (1.0 / TURN_STEPS)
    segment = spread[:, 2 * LANES : 3 * LANES]
    count = spread[:, 3 * LANES :]
    cosine, sine = turn_waves(turns)
    sample = (2 * ((out_lane & 63) >> 2) + (out_lane >> 6)).astype(F32)
    radial = (P_SIZE * segment + sample - RO // 2 + 0.5) * ((NG - 8) / RO)
    coord_x = jnp.where(sample < count, NG / 2 + radial * cosine, FAR)
    coord_y = NG / 2 + radial * sine
    coords[...] = jnp.where(is_x, coord_x, coord_y)

    big = (bins * KP * 16, LANES)
    place_row = iota(big, 0)
    place_lane = iota(big, 1)
    wanted = (CAPK * (place_row >> 4) + (place_row & 3)).astype(F32)
    hit = (wanted == jnp.broadcast_to(slot_row, big)) & (((place_row >> 2) & 3) == (place_lane >> 5))
    place = jnp.where(hit, 1.0, 0.0).astype(BF16)
    for quarter in range(4):
        for fourth in range(4):
            first = (4 * fourth + quarter) * LANES
            stacked[quarter * blocks : (quarter + 1) * blocks, fourth * LANES : (fourth + 1) * LANES] = (
                data_ref[:, first : first + LANES]
            )
    placed_rows[...] = jnp.dot(place, stacked[...], preferred_element_type=F32)

    half_lane = iota((PC, LANES), 1) < 64

    def turn_pair(pair, carry):
        base = pl.multiple_of(pair * 32, 32)
        pieces = [
            placed_rows[pl.ds(base + 16 * route, 16), fourth * LANES : (fourth + 1) * LANES]
            for route in range(2)
            for fourth in range(4)
        ]
        turned = jnp.concatenate(pieces, axis=0).T
        low, high = turned[:PC], turned[PC:]
        first = jnp.where(half_lane, low, pltpu.roll(high, 64, 1))
        second = jnp.where(half_lane, pltpu.roll(low, 64, 1), high)
        at = pl.multiple_of(pair * 2 * PC, 2 * PC)
        tiles[pl.ds(at, PC), :] = first.astype(BF16)
        tiles[pl.ds(at + PC, PC), :] = second.astype(BF16)
        return carry

    lax.fori_loop(0, bins * KP // 2, turn_pair, 0)

    pl.semaphore_wait(barrier, bins - 1)

    def tile_rows(index):
        return pl.ds(pl.multiple_of(index * ROUTE_ROWS, ROUTE_ROWS), ROUTE_ROWS)

    def coord_rows(index):
        return pl.ds(pl.multiple_of(index * 8, 8), 8)

    up = {"bin": lax.rem(me + 1, bins)}
    down = {"bin": lax.rem(me + bins - 1, bins)}
    edge_copies = [
        pltpu.make_async_remote_copy(
            image_ref, above_out, send_sems.at[2], recv_sems.at[2], down, MESH
        ),
        pltpu.make_async_remote_copy(
            image_ref, below_out, send_sems.at[3], recv_sems.at[3], up, MESH
        ),
        pltpu.make_async_remote_copy(
            weight_ref, below_weight_out, send_sems.at[4], recv_sems.at[4], up, MESH
        ),
    ]
    for step in range(1, bins):
        peer = lax.rem(me + step, bins)
        pltpu.make_async_remote_copy(
            coords.at[coord_rows(peer)],
            coords_out.at[coord_rows(me)],
            send_sems.at[0],
            recv_sems.at[0],
            {"bin": peer},
            MESH,
        ).start()
        pltpu.make_async_remote_copy(
            tiles.at[tile_rows(peer)],
            tiles_out.at[tile_rows(me)],
            send_sems.at[1],
            recv_sems.at[1],
            {"bin": peer},
            MESH,
        ).start()
    for copy in edge_copies:
        copy.start()
    own = [
        pltpu.make_async_copy(
            coords.at[coord_rows(me)], coords_out.at[coord_rows(me)], local_sems.at[0]
        ),
        pltpu.make_async_copy(
            tiles.at[tile_rows(me)], tiles_out.at[tile_rows(me)], local_sems.at[1]
        ),
    ]
    for copy in own:
        copy.start()
    for copy in own:
        copy.wait()
    others = pl.ds(0, (bins - 1) * 8)
    all_bytes(coords_out.at[others], recv_sems.at[0])
    all_bytes(coords.at[others], send_sems.at[0])
    others = pl.ds(0, (bins - 1) * ROUTE_ROWS)
    all_bytes(tiles_out.at[others], recv_sems.at[1])
    all_bytes(tiles.at[others], send_sems.at[1])
    for copy in edge_copies:
        copy.wait()


def route_samples(bins, data, routes, spokes, segments, counts, image, weight):
    any_space = pl.BlockSpec(memory_space=pl.ANY)
    vmem = pl.BlockSpec(memory_space=pltpu.VMEM)
    blocks = data.shape[0]
    route_count = bins * KP
    return pl.pallas_call(
        functools.partial(route_kernel, bins),
        out_shape=(
            jax.ShapeDtypeStruct((bins * ROUTE_ROWS, LANES), BF16),
            jax.ShapeDtypeStruct((bins * 8, LANES), F32),
            jax.ShapeDtypeStruct(image.shape, F32),
            jax.ShapeDtypeStruct(image.shape, F32),
            jax.ShapeDtypeStruct(weight.shape, F32),
        ),
        in_specs=[vmem] * 5 + [any_space] * 2,
        out_specs=(any_space,) * 5,
        scratch_shapes=[
            pltpu.VMEM((4 * blocks, 4 * LANES), BF16),
            pltpu.VMEM((route_count * 16, 4 * LANES), F32),
            pltpu.VMEM((bins * ROUTE_ROWS, LANES), BF16),
            pltpu.VMEM((bins * 8, LANES), F32),
            pltpu.SemaphoreType.DMA((2,)),
            pltpu.SemaphoreType.DMA((5,)),
            pltpu.SemaphoreType.DMA((5,)),
        ],
        compiler_params=pltpu.CompilerParams(
            collective_id=0, has_side_effects=True, vmem_limit_bytes=32 << 20
        ),
    )(data, routes, spokes, segments, counts, image, weight)


def grid_kernel(
    bins,
    slabs,
    tiles_ref,
    coords_ref,
    x_table_ref,
    z_table_ref,
    sens_hbm,
    image_ref,
    above_ref,
    below_ref,
    weight_ref,
    below_weight_ref,
    out_ref,
    samples,
    row_real,
    row_imag,
    across,
    weighted,
    sending,
    received,
    sens,
    widened,
    total,
    local_sems,
    send_sems,
    recv_sems,
):
    me = lax.axis_index("slab")
    my_bin = lax.axis_index("bin")
    barrier = pltpu.get_barrier_semaphore()

    def greet(step, carry):
        pl.semaphore_signal(
            barrier, inc=1, device_id={"slab": lax.rem(me + step, slabs)}, device_id_type=MESH
        )
        return carry

    lax.fori_loop(1, slabs, greet, 0)
    sens_copy = pltpu.make_async_copy(sens_hbm, sens, local_sems.at[0])
    sens_copy.start()

    y_offset = (iota((WY, LANES), 0) - WY // 2).astype(F32)
    taps = [turn_waves(y_offset * (m / NG)) for m in range(1, 4)]

    def prepare(step, carry):
        source = lax.rem(step, bins)
        part = lax.div(step, bins)
        rows = pl.ds(pl.multiple_of(part * PC, PC), PC)
        samples[source, rows, :] = tiles_ref[source, rows, :].astype(F32)
        coord_x = coords_ref[source, pl.ds(part, 1), :]
        coord_y = coords_ref[source, pl.ds(KP + part, 1), :]
        cell = jnp.floor(coord_y)
        ahead = coord_y - cell
        behind = 1.0 - ahead
        weights = [
            behind * behind * behind * (1.0 / 6.0),
            2.0 / 3.0 + ahead * ahead * (0.5 * ahead - 1.0),
            2.0 / 3.0 + behind * behind * (0.5 * behind - 1.0),
            ahead * ahead * ahead * (1.0 / 6.0),
        ]
        steps = y_offset * (cell - (1.0 + NG // 2))
        turns = steps * (1.0 / NG)
        base_cos, base_sin = turn_waves(turns - jnp.floor(turns))
        sum_cos = jnp.broadcast_to(weights[0], (WY, LANES))
        sum_sin = jnp.zeros((WY, LANES), F32)
        for weight, (tap_cos, tap_sin) in zip(weights[1:], taps):
            sum_cos = sum_cos + weight * tap_cos
            sum_sin = sum_sin + weight * tap_sin
        at = pl.ds(pl.multiple_of(step * WY, WY), WY)
        row_real[at, :] = sum_cos * base_cos - sum_sin * base_sin
        row_imag[at, :] = sum_cos * base_sin + sum_sin * base_cos
        lanes = pl.ds(pl.multiple_of(source * LANES, LANES), LANES)
        piece = 32
        for first in range(0, NG, piece):
            column = (iota((piece, LANES), 0) + first).astype(F32)
            across[part, first : first + piece, lanes] = spline_weight(coord_x - column).astype(BF16)
        return carry

    lax.fori_loop(0, KP * bins, prepare, 0)

    def slab_copy(group, step):
        peer = lax.rem(me + step, slabs)
        return pltpu.make_async_remote_copy(
            sending.at[group, peer],
            received.at[group, me],
            send_sems.at[group],
            recv_sems.at[group],
            {"slab": peer},
            MESH,
        )

    def own_copy(group):
        return pltpu.make_async_copy(
            sending.at[group, me], received.at[group, me], local_sems.at[1 + group]
        )

    for group in range(COIL_GROUPS):

        def grid_part(part, carry, group=group):
            def weigh(source, carry):
                at = pl.ds(pl.multiple_of((part * bins + source) * WY, WY), WY)
                real, imag = row_real[at, :], row_imag[at, :]
                lanes = pl.ds(pl.multiple_of(source * LANES, LANES), LANES)
                for coil in range(GC):
                    row = part * PC + group * GC + coil
                    data_real = samples[source, pl.ds(row, 1), :]
                    data_imag = samples[source, pl.ds(row + C, 1), :]
                    weighted[coil * WY : (coil + 1) * WY, lanes] = (
                        real * data_real - imag * data_imag
                    ).astype(BF16)
                    weighted[(GC + coil) * WY : (GC + coil + 1) * WY, lanes] = (
                        real * data_imag + imag * data_real
                    ).astype(BF16)
                return carry

            lax.fori_loop(0, bins, weigh, 0)
            lines = lax.dot_general(
                across[part],
                weighted[...],
                (((1,), (1,)), ((), ())),
                preferred_element_type=F32,
            ).astype(BF16)
            stacked = jnp.concatenate([lines[:, :LANES], lines[:, LANES:]], axis=0)
            spectra = jnp.dot(x_table_ref[...], stacked, preferred_element_type=F32)
            rows = 2 * NXI // slabs
            at = pl.ds(pl.multiple_of(part * rows, rows), rows)
            sending[group, :, at, :] = spectra.astype(BF16).reshape(slabs, rows, LANES)
            return carry

        lax.fori_loop(0, KP, grid_part, 0)
        if group == 0:
            pl.semaphore_wait(barrier, slabs - 1)

        def send(step, carry, group=group):
            slab_copy(group, step).start()
            return carry

        lax.fori_loop(1, slabs, send, 0)
        own_copy(group).start()

    sens_copy.wait()
    depth = KP * slabs
    rows = 2 * NXI // slabs
    features = GC * WY
    for group in range(COIL_GROUPS):
        own_copy(group).wait()
        others = pl.ds(0, slabs - 1)
        all_bytes(received.at[group, others], recv_sems.at[group])

        def widen(source, carry, group=group):
            at = pl.ds(source * KP, KP)
            widened[at] = received[group, source].astype(F32).reshape(KP, rows, LANES)
            return carry

        lax.fori_loop(0, slabs, widen, 0)
        for pair in range(rows // 4):
            columns = []
            for column in (2 * pair, 2 * pair + 1):
                real = widened[:, 2 * column, :].astype(BF16)
                imag = widened[:, 2 * column + 1, :].astype(BF16)
                columns.append(jnp.concatenate([real, imag], axis=0))
            images = jnp.dot(
                z_table_ref[...],
                jnp.concatenate(columns, axis=1),
                preferred_element_type=F32,
            )
            for at, column in enumerate((2 * pair, 2 * pair + 1)):
                image_real = images[:depth, at * LANES : (at + 1) * LANES]
                image_imag = images[depth:, at * LANES : (at + 1) * LANES]
                first = 2 * column * C * WY + group * features
                sens_real = sens[:, first : first + features].astype(F32)
                first = first + C * WY
                sens_imag = sens[:, first : first + features].astype(F32)
                real = sens_real * image_real + sens_imag * image_imag
                imag = sens_real * image_imag - sens_imag * image_real
                if group > 0:
                    real = real + total[2 * column]
                    imag = imag + total[2 * column + 1]
                total[2 * column] = real
                total[2 * column + 1] = imag

    for group in range(COIL_GROUPS):
        all_bytes(sending.at[group, pl.ds(0, slabs - 1)], send_sems.at[group])

    scaling = 1.0 / math.sqrt(P_SIZE * bins * BLKB * depth * C / KP)
    data_term = []
    place = iota((depth, LANES), 1) >> 4
    for half in range(rows // 8):
        line = jnp.zeros((depth, LANES), F32)
        for at in range(8):
            value = total[half * 8 + at]
            for shift in (64, 32, 16):
                value = value + pltpu.roll(value, shift, 1)
            line = jnp.where(place == at, value, line)
        data_term.append(line * scaling)
    data_term = jnp.concatenate(data_term, axis=1)

    wide = out_ref.shape[1]
    lane = iota((depth, wide), 1)
    upper_half = ((lane >> 4) & 1) == 1
    from_lane = iota((wide // 2, wide), 0)
    to_lane = iota((wide // 2, wide), 1)
    widen_weight = jnp.where(
        from_lane == ((to_lane >> 5) << 4) + (to_lane & 15), 1.0, 0.0
    )

    def edge(difference, weight):
        square = difference * difference
        other = jnp.where(
            upper_half, pltpu.roll(square, 16, 1), pltpu.roll(square, wide - 16, 1)
        )
        magnitude = jnp.sqrt(square + other + SMOOTHING * SMOOTHING)
        spread = jnp.dot(
            weight, widen_weight, preferred_element_type=F32, precision=lax.Precision.HIGHEST
        )
        return spread * difference / magnitude

    current = image_ref[...]
    own_edge = edge(above_ref[...] - current, weight_ref[...])
    below_edge = edge(current - below_ref[...], below_weight_ref[...])
    own_edge = jnp.where(my_bin == bins - 1, 0.0, own_edge)
    below_edge = jnp.where(my_bin == 0, 0.0, below_edge)
    out_ref[...] = below_edge - own_edge - data_term


def grid_and_combine(
    bins, slabs, tiles, coords, x_table, z_table, sens, image, above, below, weight, below_weight
):
    any_space = pl.BlockSpec(memory_space=pl.ANY)
    vmem = pl.BlockSpec(memory_space=pltpu.VMEM)
    depth = sens.shape[0]
    rows = 2 * NXI // slabs
    return pl.pallas_call(
        functools.partial(grid_kernel, bins, slabs),
        out_shape=jax.ShapeDtypeStruct(image.shape, F32),
        in_specs=[vmem] * 4 + [any_space] + [vmem] * 5,
        out_specs=vmem,
        scratch_shapes=[
            pltpu.VMEM((bins, ROUTE_ROWS, LANES), F32),
            pltpu.VMEM((KP * bins * WY, LANES), F32),
            pltpu.VMEM((KP * bins * WY, LANES), F32),
            pltpu.VMEM((KP, NG, bins * LANES), BF16),
            pltpu.VMEM((2 * GC * WY, bins * LANES), BF16),
            pltpu.VMEM((COIL_GROUPS, slabs, KP * rows, LANES), BF16),
            pltpu.VMEM((COIL_GROUPS, slabs, KP * rows, LANES), BF16),
            pltpu.VMEM(sens.shape, BF16),
            pltpu.VMEM((depth, rows, LANES), F32),
            pltpu.VMEM((rows, depth, LANES), F32),
            pltpu.SemaphoreType.DMA((1 + COIL_GROUPS,)),
            pltpu.SemaphoreType.DMA((COIL_GROUPS,)),
            pltpu.SemaphoreType.DMA((COIL_GROUPS,)),
        ],
        compiler_params=pltpu.CompilerParams(
            collective_id=1, has_side_effects=True, vmem_limit_bytes=48 << 20
        ),
    )(tiles, coords, x_table, z_table, sens, image, above, below, weight, below_weight)


def x_phases():
    out_index = np.arange(NXI) - NXI // 2
    in_index = np.arange(NG) - NG // 2
    angles = 2.0 * math.pi / NG * (out_index[:, None] * in_index[None, :] % NG)
    cosine, sine = np.cos(angles), np.sin(angles)
    table = np.stack(
        [np.concatenate([cosine, -sine], axis=1), np.concatenate([sine, cosine], axis=1)], axis=1
    )
    return table.reshape(2 * NXI, 2 * NG)


def z_phases(depth):
    index = np.arange(depth) - depth // 2
    angles = 2.0 * math.pi / depth * (index[:, None] * index[None, :] % depth)
    cosine, sine = np.cos(angles), np.sin(angles)
    return np.concatenate(
        [np.concatenate([cosine, -sine], axis=1), np.concatenate([sine, cosine], axis=1)], axis=0
    )


def shards(
    sample_data,
    block_route,
    spoke_index,
    segment_index,
    sample_count,
    sensitivity,
    image,
    tv_weight,
):
    bins = lax.axis_size("bin")
    slabs = lax.axis_size("slab")
    x_table = jnp.asarray(x_phases().astype(ml_dtypes.bfloat16))
    z_table = jnp.asarray(z_phases(sensitivity.shape[0]).astype(ml_dtypes.bfloat16))
    current = image[0]
    weight = tv_weight[0]
    tiles, coords, above, below, below_weight = route_samples(
        bins,
        sample_data,
        block_route,
        spoke_index.reshape(1, -1),
        segment_index.reshape(1, -1),
        sample_count.reshape(1, -1),
        current,
        weight,
    )
    gradient = grid_and_combine(
        bins,
        slabs,
        tiles.reshape(bins, ROUTE_ROWS, LANES),
        coords.reshape(bins, 8, LANES),
        x_table,
        z_table,
        sensitivity,
        current,
        above,
        below,
        weight,
        below_weight,
    )
    return gradient.reshape(image.shape)


def solution(mesh):
    return jax.shard_map(
        shards,
        mesh=mesh,
        in_specs=(
            P(("bin", "slab"), None),
            P(("bin", "slab"), None),
            P(("bin", "slab")),
            P(("bin", "slab")),
            P(("bin", "slab")),
            P(None, "slab"),
            P("bin", None, "slab"),
            P("bin", None, "slab"),
        ),
        out_specs=P("bin", None, "slab"),
        check_vma=False,
    )
```

```python
import functools
import math

import jax
import jax.numpy as jnp
import ml_dtypes
import numpy as np
from jax import lax
from jax.experimental import pallas as pl
from jax.experimental.pallas import tpu as pltpu
from jax.sharding import PartitionSpec as P

C = 32
NG = 384
NXI = 256
WY = 16
RO = 384
P_SIZE = 32
KP = 3
BLKB = 4
CAPK = 4

SMOOTHING = 0.5
GOLDEN_STEP = 40503
TURN_STEPS = 65536

F32 = jnp.float32
BF16 = jnp.bfloat16
LANES = 128
PC = 2 * C
ROUTE_ROWS = KP * PC
HALVES = 2
COIL_GROUPS = 4
GC = C // COIL_GROUPS
MESH = pl.DeviceIdType.MESH
FAR = -1000.0


def iota(shape, dim):
    return lax.broadcasted_iota(jnp.int32, shape, dim)


def turn_waves(turns):
    quarter = jnp.floor(4.0 * turns + 0.5)
    angle = (2.0 * math.pi) * (turns - 0.25 * quarter)
    sq = angle * angle
    sine = angle + angle * sq * (
        -1.0 / 6 + sq * (1.0 / 120 + sq * (-1.0 / 5040 + sq * (1.0 / 362880)))
    )
    cosine = 1.0 + sq * (
        -0.5 + sq * (1.0 / 24 + sq * (-1.0 / 720 + sq * (1.0 / 40320 + sq * (-1.0 / 3628800))))
    )
    turn = quarter - 4.0 * jnp.floor(0.25 * quarter)
    odd = (turn == 1.0) | (turn == 3.0)
    first = jnp.where(odd, sine, cosine)
    second = jnp.where(odd, cosine, sine)
    cos_out = jnp.where((turn == 1.0) | (turn == 2.0), -first, first)
    sin_out = jnp.where(turn >= 2.0, -second, second)
    return cos_out, sin_out


def spline_weight(offset):
    distance = jnp.abs(offset)
    inside = 2.0 / 3.0 + distance * distance * (0.5 * distance - 1.0)
    rest = jnp.maximum(2.0 - distance, 0.0)
    return jnp.where(distance < 1.0, inside, rest * rest * (rest * (1.0 / 6.0)))


def all_bytes(ref, sem):
    pltpu.make_async_copy(ref, ref, sem).wait()


def slab_kernel(
    bins,
    slabs,
    data_hbm,
    route_hbm,
    spoke_hbm,
    segment_hbm,
    count_hbm,
    sens_hbm,
    image_hbm,
    weight_hbm,
    x_table_hbm,
    z_table_hbm,
    out_ref,
    data,
    route,
    spoke,
    segment,
    count,
    sens,
    image,
    weight,
    x_table,
    z_table,
    stacked,
    placed_rows,
    tiles,
    coords,
    tiles_in,
    coords_in,
    above,
    below,
    own_edge,
    samples,
    row_real,
    row_imag,
    across,
    kernel_x,
    weighted,
    sending,
    received,
    widened,
    total,
    load_sems,
    own_sems,
    send_sems,
    recv_sems,
    group_send_sems,
    group_recv_sems,
):
    slab = lax.axis_index("slab")
    me = lax.axis_index("bin")
    half_slabs = slabs // HALVES
    half = lax.div(slab, half_slabs)
    place = lax.rem(slab, half_slabs)
    opposite = lax.rem(slab + half_slabs, slabs)
    sources = HALVES * bins
    parts = HALVES * KP
    depth = KP * slabs
    rows = 2 * NXI // slabs
    wide = out_ref.shape[1]
    blocks = data.shape[0]
    lanes_in = bins * LANES

    barrier = pltpu.get_barrier_semaphore()
    route_peers = [(side, step) for step in range(bins) for side in (1, 0)]
    route_peers.remove((0, 0))

    def route_peer(across_half, step):
        return {
            "bin": lax.rem(me + step, bins),
            "slab": opposite if across_half else slab,
        }

    def half_peer(step):
        return lax.rem(place + step, half_slabs)

    for pair in route_peers:
        pl.semaphore_signal(barrier, inc=1, device_id=route_peer(*pair), device_id_type=MESH)
    for step in range(1, half_slabs):
        pl.semaphore_signal(
            barrier,
            inc=1,
            device_id={"slab": half * half_slabs + half_peer(step)},
            device_id_type=MESH,
        )

    loads = [
        pltpu.make_async_copy(from_ref, to_ref, load_sems.at[at])
        for at, (from_ref, to_ref) in enumerate(
            [
                (route_hbm, route),
                (spoke_hbm, spoke),
                (segment_hbm, segment),
                (count_hbm, count),
                (data_hbm, data),
                (image_hbm, image),
                (weight_hbm, weight),
                (x_table_hbm.at[half], x_table),
                (z_table_hbm, z_table),
                (sens_hbm, sens),
            ]
        )
    ]
    for copy in loads:
        copy.start()
    for copy in loads[:4]:
        copy.wait()

    row = iota((blocks, LANES), 0)
    lane = iota((blocks, LANES), 1)
    lane_block = lane & (blocks - 1)

    def column(ref_row):
        spread = jnp.broadcast_to(ref_row.astype(F32), (blocks, blocks))
        eye = iota((blocks, blocks), 0) == iota((blocks, blocks), 1)
        return jnp.sum(jnp.where(eye, spread, 0.0), axis=1, keepdims=True)

    route_col = jnp.broadcast_to(column(route[...]), (blocks, LANES))
    route_row = jnp.sum(jnp.where(row == lane_block, route_col, 0.0), axis=0, keepdims=True)
    same = route_col == jnp.broadcast_to(route_row, (blocks, LANES))
    rank_row = jnp.sum(jnp.where(same & (row < lane_block), 1.0, 0.0), axis=0, keepdims=True)
    rank_col = jnp.sum(jnp.where(same & (lane < row), 1.0, 0.0), axis=1, keepdims=True)
    slot_row = route_row * CAPK + rank_row

    turn_row = (spoke[...] * GOLDEN_STEP) & (TURN_STEPS - 1)
    columns = [column(turn_row >> 8), column(turn_row & 255), column(segment[...]), column(count[...])]
    slot_hit = rank_col == (lane & (CAPK - 1)).astype(F32)
    picks = [jnp.where(slot_hit, value, 0.0) for value in columns]
    picks = jnp.concatenate(picks, axis=1).astype(BF16)
    picks = jnp.concatenate(
        [picks, jnp.zeros((LANES - blocks, len(columns) * LANES), BF16)], axis=0
    )
    coord_shape = (8 * bins, LANES)
    out_row = iota(coord_shape, 0)
    out_lane = iota(coord_shape, 1)
    part_row = out_row & 7
    is_x = part_row < KP
    partition = jnp.where(is_x, part_row, part_row - KP)
    row_route = jnp.where(part_row < 2 * KP, KP * (out_row >> 3) + partition, -1).astype(F32)
    chosen = (row_route == jnp.broadcast_to(route_row, coord_shape)) & (out_lane < blocks)
    spread = jnp.dot(jnp.where(chosen, 1.0, 0.0).astype(BF16), picks, preferred_element_type=F32)
    turns = (256.0 * spread[:, :LANES] + spread[:, LANES : 2 * LANES]) * (1.0 / TURN_STEPS)
    cosine, sine = turn_waves(turns)
    sample = (2 * ((out_lane & 63) >> 2) + (out_lane >> 6)).astype(F32)
    radial = (P_SIZE * spread[:, 2 * LANES : 3 * LANES] + sample - RO // 2 + 0.5) * ((NG - 8) / RO)
    coord_x = jnp.where(sample < spread[:, 3 * LANES :], NG / 2 + radial * cosine, FAR)
    coord_y = NG / 2 + radial * sine
    coords[...] = jnp.where(is_x, coord_x, coord_y)

    def coord_rows(index):
        return pl.ds(pl.multiple_of(index * 8, 8), 8)

    def tile_rows(index):
        return pl.ds(pl.multiple_of(index * ROUTE_ROWS, ROUTE_ROWS), ROUTE_ROWS)

    my_source = half * bins + me
    image_copy = pltpu.make_async_remote_copy(
        image,
        above,
        send_sems.at[2],
        recv_sems.at[2],
        {"bin": lax.rem(me + bins - 1, bins)},
        MESH,
    )
    edge_copy = pltpu.make_async_remote_copy(
        own_edge, below, send_sems.at[3], recv_sems.at[3], {"bin": lax.rem(me + 1, bins)}, MESH
    )
    is_first = me == 0
    is_last = me == bins - 1
    loads[5].wait()
    pl.semaphore_wait(barrier, len(route_peers) + half_slabs - 1)

    @pl.when(jnp.logical_not(is_first))
    def _():
        image_copy.start()

    for pair in route_peers:
        peer = route_peer(*pair)
        pltpu.make_async_remote_copy(
            coords.at[coord_rows(peer["bin"])],
            coords_in.at[coord_rows(my_source)],
            send_sems.at[0],
            recv_sems.at[0],
            peer,
            MESH,
        ).start()
    own_coords = pltpu.make_async_copy(
        coords.at[coord_rows(me)], coords_in.at[coord_rows(my_source)], own_sems.at[0]
    )
    own_coords.start()

    loads[4].wait()
    big = (bins * KP * 16, LANES)
    place_row = iota(big, 0)
    place_lane = iota(big, 1)
    wanted = (CAPK * (place_row >> 4) + (place_row & 3)).astype(F32)
    hit = (wanted == jnp.broadcast_to(slot_row, big)) & (((place_row >> 2) & 3) == (place_lane >> 5))
    one_hot = jnp.where(hit, 1.0, 0.0).astype(BF16)
    for quarter in range(4):
        for fourth in range(4):
            first = (4 * fourth + quarter) * LANES
            to_rows = slice(quarter * blocks, (quarter + 1) * blocks)
            stacked[to_rows, fourth * LANES : (fourth + 1) * LANES] = data[:, first : first + LANES]
    placed_rows[...] = jnp.dot(one_hot, stacked[...], preferred_element_type=F32)
    half_lane = iota((PC, LANES), 1) < 64

    def turn_pair(pair, carry):
        base = pl.multiple_of(pair * 32, 32)
        pieces = [
            placed_rows[pl.ds(base + 16 * one, 16), fourth * LANES : (fourth + 1) * LANES]
            for one in range(2)
            for fourth in range(4)
        ]
        turned = jnp.concatenate(pieces, axis=0).T
        low, high = turned[:PC], turned[PC:]
        at = pl.multiple_of(pair * 2 * PC, 2 * PC)
        tiles[pl.ds(at, PC), :] = jnp.where(half_lane, low, pltpu.roll(high, 64, 1)).astype(BF16)
        tiles[pl.ds(at + PC, PC), :] = jnp.where(half_lane, pltpu.roll(low, 64, 1), high).astype(BF16)
        return carry

    lax.fori_loop(0, bins * KP // 2, turn_pair, 0)
    for pair in route_peers:
        peer = route_peer(*pair)
        pltpu.make_async_remote_copy(
            tiles.at[tile_rows(peer["bin"])],
            tiles_in.at[tile_rows(my_source)],
            send_sems.at[1],
            recv_sems.at[1],
            peer,
            MESH,
        ).start()
    own_tiles = pltpu.make_async_copy(
        tiles.at[tile_rows(me)], tiles_in.at[tile_rows(my_source)], own_sems.at[1]
    )
    own_tiles.start()

    own_coords.wait()
    others = pl.ds(0, (sources - 1) * 8)
    all_bytes(coords_in.at[others], recv_sems.at[0])
    loads[7].wait()
    y_offset = (iota((WY, LANES), 0) - WY // 2).astype(F32)
    taps = [turn_waves(y_offset * (m / NG)) for m in range(1, 4)]

    def prepare(step, carry):
        side = lax.div(step, KP)
        part = lax.rem(step, KP)

        def prepare_source(source, carry):
            base = pl.multiple_of((side * bins + source) * 8, 8)
            coord_x = coords_in[pl.ds(base + part, 1), :]
            coord_y = coords_in[pl.ds(base + KP + part, 1), :]
            cell = jnp.floor(coord_y)
            ahead = coord_y - cell
            behind = 1.0 - ahead
            weights = [
                behind * behind * behind * (1.0 / 6.0),
                2.0 / 3.0 + ahead * ahead * (0.5 * ahead - 1.0),
                2.0 / 3.0 + behind * behind * (0.5 * behind - 1.0),
                ahead * ahead * ahead * (1.0 / 6.0),
            ]
            steps = y_offset * (cell - (1.0 + NG // 2))
            base_turns = steps * (1.0 / NG)
            base_cos, base_sin = turn_waves(base_turns - jnp.floor(base_turns))
            sum_cos = jnp.broadcast_to(weights[0], (WY, LANES))
            sum_sin = jnp.zeros((WY, LANES), F32)
            for tap_weight, (tap_cos, tap_sin) in zip(weights[1:], taps):
                sum_cos = sum_cos + tap_weight * tap_cos
                sum_sin = sum_sin + tap_weight * tap_sin
            at = pl.ds(pl.multiple_of((step * bins + source) * WY, WY), WY)
            row_real[at, :] = sum_cos * base_cos - sum_sin * base_sin
            row_imag[at, :] = sum_cos * base_sin + sum_sin * base_cos
            lanes = pl.ds(pl.multiple_of(source * LANES, LANES), LANES)
            piece = 32
            for first in range(0, NG, piece):
                cells = (iota((piece, LANES), 0) + first).astype(F32)
                across[first : first + piece, lanes] = spline_weight(coord_x - cells).astype(BF16)
            return carry

        lax.fori_loop(0, bins, prepare_source, 0)
        kernel_x[step] = jnp.dot(x_table[...], across[...], preferred_element_type=F32).astype(BF16)
        return carry

    lax.fori_loop(0, parts, prepare, 0)

    loads[6].wait()

    @pl.when(jnp.logical_not(is_last))
    def _():
        image_copy.wait_recv()

    @pl.when(is_last)
    def _():
        above[...] = image[...]

    lane = iota((depth, wide), 1)
    upper_half = ((lane >> 4) & 1) == 1
    from_lane = iota((wide // 2, wide), 0)
    to_lane = iota((wide // 2, wide), 1)
    widen_weight = jnp.where(from_lane == ((to_lane >> 5) << 4) + (to_lane & 15), 1.0, 0.0)
    difference = above[...] - image[...]
    square = difference * difference
    other = jnp.where(upper_half, pltpu.roll(square, 16, 1), pltpu.roll(square, wide - 16, 1))
    magnitude = jnp.sqrt(square + other + SMOOTHING * SMOOTHING)
    wide_weight = jnp.dot(
        weight[...], widen_weight, preferred_element_type=F32, precision=lax.Precision.HIGHEST
    )
    own_edge[...] = wide_weight * difference / magnitude

    @pl.when(jnp.logical_not(is_last))
    def _():
        edge_copy.start()

    @pl.when(is_first)
    def _():
        below[...] = jnp.zeros_like(below)

    own_tiles.wait()
    others = pl.ds(0, (sources - 1) * ROUTE_ROWS)
    all_bytes(tiles_in.at[others], recv_sems.at[1])

    def widen_samples(source, carry):
        samples[source] = tiles_in[tile_rows(source), :].astype(F32)
        return carry

    lax.fori_loop(0, sources, widen_samples, 0)

    def own_copy(group):
        return pltpu.make_async_copy(
            sending.at[group, place], received.at[group, place], own_sems.at[2 + group]
        )

    for group in range(COIL_GROUPS):

        def grid_part(step, carry, group=group):
            side = lax.div(step, KP)
            part = lax.rem(step, KP)

            def weigh(source, carry):
                at = pl.ds(pl.multiple_of((step * bins + source) * WY, WY), WY)
                real, imag = row_real[at, :], row_imag[at, :]
                lanes = pl.ds(pl.multiple_of(source * LANES, LANES), LANES)
                for coil in range(GC):
                    at_row = part * PC + group * GC + coil
                    data_real = samples[side * bins + source, pl.ds(at_row, 1), :]
                    data_imag = samples[side * bins + source, pl.ds(at_row + C, 1), :]
                    weighted[coil * WY : (coil + 1) * WY, lanes] = (
                        real * data_real - imag * data_imag
                    ).astype(BF16)
                    weighted[(GC + coil) * WY : (GC + coil + 1) * WY, lanes] = (
                        real * data_imag + imag * data_real
                    ).astype(BF16)
                return carry

            lax.fori_loop(0, bins, weigh, 0)
            products = lax.dot_general(
                kernel_x[step],
                weighted[...],
                (((1,), (1,)), ((), ())),
                preferred_element_type=F32,
            )
            count_x = NXI // HALVES
            real = products[:count_x, :LANES] - products[count_x:, LANES:]
            imag = products[:count_x, LANES:] + products[count_x:, :LANES]
            shape = (half_slabs, rows // 2, LANES)
            spectra = jnp.concatenate([real.reshape(shape), imag.reshape(shape)], axis=1)
            at = pl.ds(pl.multiple_of(step * rows, rows), rows)
            sending[group, :, at, :] = spectra.astype(BF16)
            return carry

        lax.fori_loop(0, parts, grid_part, 0)
        for step in range(1, half_slabs):
            peer = half_peer(step)
            pltpu.make_async_remote_copy(
                sending.at[group, peer],
                received.at[group, place],
                group_send_sems.at[group],
                group_recv_sems.at[group],
                {"slab": half * half_slabs + peer},
                MESH,
            ).start()
        own_copy(group).start()

    loads[8].wait()
    loads[9].wait()
    features = GC * WY
    for group in range(COIL_GROUPS):
        own_copy(group).wait()
        others = pl.ds(0, half_slabs - 1)
        all_bytes(received.at[group, others], group_recv_sems.at[group])

        def widen(source, carry, group=group):
            at = pl.ds(source * parts, parts)
            widened[at] = received[group, source].astype(F32).reshape(parts, rows, LANES)
            return carry

        lax.fori_loop(0, half_slabs, widen, 0)
        for pair in range(rows // 4):
            inputs = []
            for at_x in (2 * pair, 2 * pair + 1):
                real = widened[:, at_x, :].astype(BF16)
                imag = widened[:, rows // 2 + at_x, :].astype(BF16)
                inputs.append(jnp.concatenate([real, imag], axis=0))
            images = jnp.dot(
                z_table[...], jnp.concatenate(inputs, axis=1), preferred_element_type=F32
            )
            for at, at_x in enumerate((2 * pair, 2 * pair + 1)):
                image_real = images[:depth, at * LANES : (at + 1) * LANES]
                image_imag = images[depth:, at * LANES : (at + 1) * LANES]
                first = 2 * at_x * C * WY + group * features
                sens_real = sens[:, first : first + features].astype(F32)
                first = first + C * WY
                sens_imag = sens[:, first : first + features].astype(F32)
                real = sens_real * image_real + sens_imag * image_imag
                imag = sens_real * image_imag - sens_imag * image_real
                if group > 0:
                    real = real + total[2 * at_x]
                    imag = imag + total[2 * at_x + 1]
                total[2 * at_x] = real
                total[2 * at_x + 1] = imag

    others = pl.ds(0, half_slabs - 1)
    for group in range(COIL_GROUPS):
        all_bytes(sending.at[group, others], group_send_sems.at[group])
    all_bytes(coords_in.at[pl.ds(0, (sources - 1) * 8)], send_sems.at[0])
    all_bytes(tiles_in.at[pl.ds(0, (sources - 1) * ROUTE_ROWS)], send_sems.at[1])

    @pl.when(jnp.logical_not(is_first))
    def _():
        image_copy.wait_send()
        edge_copy.wait_recv()

    @pl.when(jnp.logical_not(is_last))
    def _():
        edge_copy.wait_send()

    scaling = 1.0 / math.sqrt(P_SIZE * bins * BLKB * depth * C / KP)
    octet = iota((depth, LANES), 1) >> 4
    for part in range(rows // 8):
        line = jnp.zeros((depth, LANES), F32)
        for at in range(8):
            value = total[part * 8 + at]
            for shift in (64, 32, 16):
                value = value + pltpu.roll(value, shift, 1)
            line = jnp.where(octet == at, value, line)
        lanes = slice(part * LANES, (part + 1) * LANES)
        out_ref[:, lanes] = below[:, lanes] - own_edge[:, lanes] - line * scaling


def slab_gradient(
    bins, slabs, data, route, spoke, segment, count, sens, image, weight, x_table, z_table
):
    hbm = pl.BlockSpec(memory_space=pltpu.HBM)
    depth = sens.shape[0]
    blocks = data.shape[0]
    rows = 2 * NXI // slabs
    sources = HALVES * bins
    parts = HALVES * KP
    half_slabs = slabs // HALVES
    operands = (data, route, spoke, segment, count, sens, image, weight, x_table, z_table)
    held = operands[:8] + (x_table[0], z_table)
    return pl.pallas_call(
        functools.partial(slab_kernel, bins, slabs),
        out_shape=jax.ShapeDtypeStruct(image.shape, F32),
        in_specs=[hbm] * len(operands),
        out_specs=pl.BlockSpec(memory_space=pltpu.VMEM),
        scratch_shapes=[pltpu.VMEM(array.shape, array.dtype) for array in held]
        + [
            pltpu.VMEM((4 * blocks, 4 * LANES), BF16),
            pltpu.VMEM((bins * KP * 16, 4 * LANES), F32),
            pltpu.VMEM((bins * ROUTE_ROWS, LANES), BF16),
            pltpu.VMEM((bins * 8, LANES), F32),
            pltpu.VMEM((sources * ROUTE_ROWS, LANES), BF16),
            pltpu.VMEM((sources * 8, LANES), F32),
            pltpu.VMEM(image.shape, F32),
            pltpu.VMEM(image.shape, F32),
            pltpu.VMEM(image.shape, F32),
            pltpu.VMEM((sources, ROUTE_ROWS, LANES), F32),
            pltpu.VMEM((parts * bins * WY, LANES), F32),
            pltpu.VMEM((parts * bins * WY, LANES), F32),
            pltpu.VMEM((NG, bins * LANES), BF16),
            pltpu.VMEM((parts, 2 * NXI // HALVES, bins * LANES), BF16),
            pltpu.VMEM((2 * GC * WY, bins * LANES), BF16),
            pltpu.VMEM((COIL_GROUPS, half_slabs, parts * rows, LANES), BF16),
            pltpu.VMEM((COIL_GROUPS, half_slabs, parts * rows, LANES), BF16),
            pltpu.VMEM((depth, rows, LANES), F32),
            pltpu.VMEM((rows, depth, LANES), F32),
            pltpu.SemaphoreType.DMA((len(operands),)),
            pltpu.SemaphoreType.DMA((2 + COIL_GROUPS,)),
            pltpu.SemaphoreType.DMA((4,)),
            pltpu.SemaphoreType.DMA((4,)),
            pltpu.SemaphoreType.DMA((COIL_GROUPS,)),
            pltpu.SemaphoreType.DMA((COIL_GROUPS,)),
        ],
        compiler_params=pltpu.CompilerParams(
            collective_id=0, has_side_effects=True, vmem_limit_bytes=48 << 20
        ),
    )(*operands)


def waves(out_index, in_index, modulus):
    angles = 2.0 * math.pi / modulus * (out_index[:, None] * in_index[None, :] % modulus)
    return np.cos(angles), np.sin(angles)


def x_phases():
    cosine, sine = waves(np.arange(NXI) - NXI // 2, np.arange(NG) - NG // 2, NG)
    shape = (HALVES, NXI // HALVES, NG)
    return np.concatenate([cosine.reshape(shape), sine.reshape(shape)], axis=1)


def z_phases(slabs):
    depth = KP * slabs
    order = np.arange(depth).reshape(HALVES, slabs // HALVES, KP).transpose(1, 0, 2).reshape(-1)
    cosine, sine = waves(np.arange(depth) - depth // 2, order - depth // 2, depth)
    return np.concatenate(
        [np.concatenate([cosine, -sine], axis=1), np.concatenate([sine, cosine], axis=1)], axis=0
    )


def shards(
    sample_data,
    block_route,
    spoke_index,
    segment_index,
    sample_count,
    sensitivity,
    image,
    tv_weight,
):
    bins = lax.axis_size("bin")
    slabs = lax.axis_size("slab")
    gradient = slab_gradient(
        bins,
        slabs,
        sample_data,
        block_route.reshape(1, -1),
        spoke_index.reshape(1, -1),
        segment_index.reshape(1, -1),
        sample_count.reshape(1, -1),
        sensitivity,
        image[0],
        tv_weight[0],
        jnp.asarray(x_phases().astype(ml_dtypes.bfloat16)),
        jnp.asarray(z_phases(slabs).astype(ml_dtypes.bfloat16)),
    )
    return gradient.reshape(image.shape)


def solution(mesh):
    return jax.shard_map(
        shards,
        mesh=mesh,
        in_specs=(
            P(("bin", "slab"), None),
            P(("bin", "slab"), None),
            P(("bin", "slab")),
            P(("bin", "slab")),
            P(("bin", "slab")),
            P(None, "slab"),
            P("bin", None, "slab"),
            P("bin", None, "slab"),
        ),
        out_specs=P("bin", None, "slab"),
        check_vma=False,
    )
```

```python
import functools
import math

import jax
import jax.numpy as jnp
import ml_dtypes
import numpy as np
from jax import lax
from jax.experimental import pallas as pl
from jax.experimental.pallas import tpu as pltpu
from jax.sharding import PartitionSpec as P

C = 32
NG = 384
NXI = 256
WY = 16
RO = 384
P_SIZE = 32
KP = 3
BLKB = 4
CAPK = 4

SMOOTHING = 0.5
GOLDEN_STEP = 40503
TURN_STEPS = 65536

F32 = jnp.float32
BF16 = jnp.bfloat16
LANES = 128
PC = 2 * C
ROUTE_ROWS = KP * PC
HALVES = 2
COIL_GROUPS = 4
GC = C // COIL_GROUPS
MESH = pl.DeviceIdType.MESH
FAR = -1000.0


def iota(shape, dim):
    return lax.broadcasted_iota(jnp.int32, shape, dim)


def turn_waves(turns):
    quarter = jnp.floor(4.0 * turns + 0.5)
    angle = (2.0 * math.pi) * (turns - 0.25 * quarter)
    sq = angle * angle
    sine = angle + angle * sq * (
        -1.0 / 6 + sq * (1.0 / 120 + sq * (-1.0 / 5040 + sq * (1.0 / 362880)))
    )
    cosine = 1.0 + sq * (
        -0.5 + sq * (1.0 / 24 + sq * (-1.0 / 720 + sq * (1.0 / 40320 + sq * (-1.0 / 3628800))))
    )
    turn = quarter - 4.0 * jnp.floor(0.25 * quarter)
    odd = (turn == 1.0) | (turn == 3.0)
    first = jnp.where(odd, sine, cosine)
    second = jnp.where(odd, cosine, sine)
    cos_out = jnp.where((turn == 1.0) | (turn == 2.0), -first, first)
    sin_out = jnp.where(turn >= 2.0, -second, second)
    return cos_out, sin_out


def spline_weight(offset):
    distance = jnp.abs(offset)
    inside = 2.0 / 3.0 + distance * distance * (0.5 * distance - 1.0)
    rest = jnp.maximum(2.0 - distance, 0.0)
    return jnp.where(distance < 1.0, inside, rest * rest * (rest * (1.0 / 6.0)))


def all_bytes(ref, sem):
    pltpu.make_async_copy(ref, ref, sem).wait()


def slab_kernel(
    bins,
    slabs,
    data_hbm,
    route_hbm,
    spoke_hbm,
    segment_hbm,
    count_hbm,
    sens_hbm,
    image_hbm,
    weight_hbm,
    x_table_hbm,
    z_table_hbm,
    out_ref,
    data,
    route,
    spoke,
    segment,
    count,
    sens,
    image,
    weight,
    x_table,
    z_table,
    stacked,
    placed_rows,
    tiles,
    coords,
    tiles_in,
    coords_in,
    above,
    below,
    own_edge,
    samples,
    row_real,
    row_imag,
    across,
    kernel_x,
    weighted,
    products,
    sending,
    received,
    widened,
    total,
    fold,
    load_sems,
    own_sems,
    send_sems,
    recv_sems,
    tile_send_sems,
    tile_recv_sems,
    group_send_sems,
    group_recv_sems,
):
    slab = lax.axis_index("slab")
    me = lax.axis_index("bin")
    half_slabs = slabs // HALVES
    half = lax.div(slab, half_slabs)
    place = lax.rem(slab, half_slabs)
    opposite = lax.rem(slab + half_slabs, slabs)
    sources = HALVES * bins
    parts = HALVES * KP
    depth = KP * slabs
    rows = 2 * NXI // slabs
    wide = out_ref.shape[1]
    blocks = data.shape[0]

    barrier = pltpu.get_barrier_semaphore()
    route_peers = [(side, step) for step in range(bins) for side in (1, 0)]
    route_peers.remove((0, 0))

    def route_peer(across_half, step):
        return {
            "bin": lax.rem(me + step, bins),
            "slab": opposite if across_half else slab,
        }

    def half_peer(step):
        return lax.rem(place + step, half_slabs)

    for pair in route_peers:
        pl.semaphore_signal(barrier, inc=1, device_id=route_peer(*pair), device_id_type=MESH)
    for step in range(1, half_slabs):
        pl.semaphore_signal(
            barrier,
            inc=1,
            device_id={"slab": half * half_slabs + half_peer(step)},
            device_id_type=MESH,
        )

    loads = [
        pltpu.make_async_copy(from_ref, to_ref, load_sems.at[at])
        for at, (from_ref, to_ref) in enumerate(
            [
                (route_hbm, route),
                (spoke_hbm, spoke),
                (segment_hbm, segment),
                (count_hbm, count),
                (data_hbm, data),
                (image_hbm, image),
                (weight_hbm, weight),
                (x_table_hbm.at[half], x_table),
                (z_table_hbm, z_table),
                (sens_hbm, sens),
            ]
        )
    ]
    for copy in loads:
        copy.start()
    for copy in loads[:4]:
        copy.wait()

    row = iota((blocks, LANES), 0)
    lane = iota((blocks, LANES), 1)
    lane_block = lane & (blocks - 1)

    def column(ref_row):
        spread = jnp.broadcast_to(ref_row.astype(F32), (blocks, blocks))
        eye = iota((blocks, blocks), 0) == iota((blocks, blocks), 1)
        return jnp.sum(jnp.where(eye, spread, 0.0), axis=1, keepdims=True)

    route_col = jnp.broadcast_to(column(route[...]), (blocks, LANES))
    route_row = jnp.sum(jnp.where(row == lane_block, route_col, 0.0), axis=0, keepdims=True)
    same = route_col == jnp.broadcast_to(route_row, (blocks, LANES))
    rank_row = jnp.sum(jnp.where(same & (row < lane_block), 1.0, 0.0), axis=0, keepdims=True)
    rank_col = jnp.sum(jnp.where(same & (lane < row), 1.0, 0.0), axis=1, keepdims=True)
    slot_row = route_row * CAPK + rank_row

    turn_row = (spoke[...] * GOLDEN_STEP) & (TURN_STEPS - 1)
    columns = [column(turn_row >> 8), column(turn_row & 255), column(segment[...]), column(count[...])]
    slot_hit = rank_col == (lane & (CAPK - 1)).astype(F32)
    picks = [jnp.where(slot_hit, value, 0.0) for value in columns]
    picks = jnp.concatenate(picks, axis=1).astype(BF16)
    picks = jnp.concatenate(
        [picks, jnp.zeros((LANES - blocks, len(columns) * LANES), BF16)], axis=0
    )
    coord_shape = (8 * bins, LANES)
    out_row = iota(coord_shape, 0)
    out_lane = iota(coord_shape, 1)
    part_row = out_row & 7
    is_x = part_row < KP
    partition = jnp.where(is_x, part_row, part_row - KP)
    row_route = jnp.where(part_row < 2 * KP, KP * (out_row >> 3) + partition, -1).astype(F32)
    chosen = (row_route == jnp.broadcast_to(route_row, coord_shape)) & (out_lane < blocks)
    spread = jnp.dot(jnp.where(chosen, 1.0, 0.0).astype(BF16), picks, preferred_element_type=F32)
    turns = (256.0 * spread[:, :LANES] + spread[:, LANES : 2 * LANES]) * (1.0 / TURN_STEPS)
    cosine, sine = turn_waves(turns)
    sample = (2 * ((out_lane & 63) >> 2) + (out_lane >> 6)).astype(F32)
    radial = (P_SIZE * spread[:, 2 * LANES : 3 * LANES] + sample - RO // 2 + 0.5) * ((NG - 8) / RO)
    coord_x = jnp.where(sample < spread[:, 3 * LANES :], NG / 2 + radial * cosine, FAR)
    coord_y = NG / 2 + radial * sine
    coords[...] = jnp.where(is_x, coord_x, coord_y)

    def coord_rows(index):
        return pl.ds(pl.multiple_of(index * 8, 8), 8)

    def tile_rows(index, many=1):
        return pl.ds(pl.multiple_of(index * PC, PC), many * PC)

    my_source = half * bins + me
    image_copy = pltpu.make_async_remote_copy(
        image,
        above,
        send_sems.at[1],
        recv_sems.at[1],
        {"bin": lax.rem(me + bins - 1, bins)},
        MESH,
    )
    edge_copy = pltpu.make_async_remote_copy(
        own_edge, below, send_sems.at[2], recv_sems.at[2], {"bin": lax.rem(me + 1, bins)}, MESH
    )
    is_first = me == 0
    is_last = me == bins - 1
    loads[5].wait()
    pl.semaphore_wait(barrier, len(route_peers) + half_slabs - 1)

    @pl.when(jnp.logical_not(is_first))
    def _():
        image_copy.start()

    for pair in route_peers:
        peer = route_peer(*pair)
        pltpu.make_async_remote_copy(
            coords.at[coord_rows(peer["bin"])],
            coords_in.at[coord_rows(my_source)],
            send_sems.at[0],
            recv_sems.at[0],
            peer,
            MESH,
        ).start()
    own_coords = pltpu.make_async_copy(
        coords.at[coord_rows(me)], coords_in.at[coord_rows(my_source)], own_sems.at[0]
    )
    own_coords.start()

    loads[4].wait()
    big = (bins * KP * 16, LANES)
    place_row = iota(big, 0)
    place_lane = iota(big, 1)
    wanted = (CAPK * (place_row >> 4) + (place_row & 3)).astype(F32)
    hit = (wanted == jnp.broadcast_to(slot_row, big)) & (((place_row >> 2) & 3) == (place_lane >> 5))
    one_hot = jnp.where(hit, 1.0, 0.0).astype(BF16)
    for quarter in range(4):
        for fourth in range(4):
            first = (4 * fourth + quarter) * LANES
            to_rows = slice(quarter * blocks, (quarter + 1) * blocks)
            stacked[to_rows, fourth * LANES : (fourth + 1) * LANES] = data[:, first : first + LANES]
    placed_rows[...] = jnp.dot(one_hot, stacked[...], preferred_element_type=F32)
    half_lane = iota((PC, LANES), 1) < 64

    def turn_pair(pair, carry):
        base = pl.multiple_of(pair * 32, 32)
        pieces = [
            placed_rows[pl.ds(base + 16 * one, 16), fourth * LANES : (fourth + 1) * LANES]
            for one in range(2)
            for fourth in range(4)
        ]
        turned = jnp.concatenate(pieces, axis=0).T
        low, high = turned[:PC], turned[PC:]
        at = pl.multiple_of(pair * 2 * PC, 2 * PC)
        tiles[pl.ds(at, PC), :] = jnp.where(half_lane, low, pltpu.roll(high, 64, 1)).astype(BF16)
        tiles[pl.ds(at + PC, PC), :] = jnp.where(half_lane, pltpu.roll(low, 64, 1), high).astype(BF16)
        return carry

    lax.fori_loop(0, bins * KP // 2, turn_pair, 0)
    own_tiles = []
    for part in range(KP):
        slot = part * sources + my_source
        for pair in route_peers:
            peer = route_peer(*pair)
            pltpu.make_async_remote_copy(
                tiles.at[tile_rows(peer["bin"] * KP + part)],
                tiles_in.at[tile_rows(slot)],
                tile_send_sems.at[part],
                tile_recv_sems.at[part],
                peer,
                MESH,
            ).start()
        copy = pltpu.make_async_copy(
            tiles.at[tile_rows(me * KP + part)], tiles_in.at[tile_rows(slot)], own_sems.at[1 + part]
        )
        copy.start()
        own_tiles.append(copy)

    fold_row = iota(fold.shape, 0)
    fold_lane = iota(fold.shape, 1)
    folds = ((fold_lane >> 4) == (fold_row >> 7)) & ((fold_lane & 15) == (fold_row & 15))
    fold[...] = jnp.where(folds, 1.0, 0.0).astype(BF16)

    own_coords.wait()
    others = pl.ds(0, (sources - 1) * 8)
    all_bytes(coords_in.at[others], recv_sems.at[0])
    loads[7].wait()
    y_offset = (iota((WY, LANES), 0) - WY // 2).astype(F32)
    taps = [turn_waves(y_offset * (m / NG)) for m in range(1, 4)]

    def prepare(step, carry):
        side = lax.div(step, KP)
        part = lax.rem(step, KP)

        def prepare_source(source, carry):
            base = pl.multiple_of((side * bins + source) * 8, 8)
            coord_x = coords_in[pl.ds(base + part, 1), :]
            coord_y = coords_in[pl.ds(base + KP + part, 1), :]
            cell = jnp.floor(coord_y)
            ahead = coord_y - cell
            behind = 1.0 - ahead
            weights = [
                behind * behind * behind * (1.0 / 6.0),
                2.0 / 3.0 + ahead * ahead * (0.5 * ahead - 1.0),
                2.0 / 3.0 + behind * behind * (0.5 * behind - 1.0),
                ahead * ahead * ahead * (1.0 / 6.0),
            ]
            steps = y_offset * (cell - (1.0 + NG // 2))
            base_turns = steps * (1.0 / NG)
            base_cos, base_sin = turn_waves(base_turns - jnp.floor(base_turns))
            sum_cos = jnp.broadcast_to(weights[0], (WY, LANES))
            sum_sin = jnp.zeros((WY, LANES), F32)
            for tap_weight, (tap_cos, tap_sin) in zip(weights[1:], taps):
                sum_cos = sum_cos + tap_weight * tap_cos
                sum_sin = sum_sin + tap_weight * tap_sin
            at = pl.ds(pl.multiple_of((step * bins + source) * WY, WY), WY)
            row_real[at, :] = sum_cos * base_cos - sum_sin * base_sin
            row_imag[at, :] = sum_cos * base_sin + sum_sin * base_cos
            lanes = pl.ds(pl.multiple_of(source * LANES, LANES), LANES)
            turned = jnp.broadcast_to(coord_x, (LANES, LANES)).T
            for first in range(0, NG, LANES):
                cells = (iota((LANES, LANES), 1) + first).astype(F32)
                across[lanes, first : first + LANES] = spline_weight(turned - cells).astype(BF16)
            return carry

        lax.fori_loop(0, bins, prepare_source, 0)
        kernel_x[step] = jnp.dot(across[...], x_table[...], preferred_element_type=F32).astype(BF16)
        return carry

    lax.fori_loop(0, parts, prepare, 0)

    loads[6].wait()

    @pl.when(jnp.logical_not(is_last))
    def _():
        image_copy.wait_recv()

    @pl.when(is_last)
    def _():
        above[...] = image[...]

    lane = iota((depth, wide), 1)
    upper_half = ((lane >> 4) & 1) == 1
    from_lane = iota((wide // 2, wide), 0)
    to_lane = iota((wide // 2, wide), 1)
    widen_weight = jnp.where(from_lane == ((to_lane >> 5) << 4) + (to_lane & 15), 1.0, 0.0)
    difference = above[...] - image[...]
    square = difference * difference
    other = jnp.where(upper_half, pltpu.roll(square, 16, 1), pltpu.roll(square, wide - 16, 1))
    magnitude = jnp.sqrt(square + other + SMOOTHING * SMOOTHING)
    wide_weight = jnp.dot(
        weight[...], widen_weight, preferred_element_type=F32, precision=lax.Precision.HIGHEST
    )
    own_edge[...] = wide_weight * difference / magnitude

    @pl.when(jnp.logical_not(is_last))
    def _():
        edge_copy.start()

    @pl.when(is_first)
    def _():
        below[...] = jnp.zeros_like(below)

    def own_copy(group):
        return pltpu.make_async_copy(
            sending.at[group, place], received.at[group, place], own_sems.at[1 + KP + group]
        )

    def take_tiles(part):
        own_tiles[part].wait()
        others = tile_rows(part * sources, sources - 1)
        all_bytes(tiles_in.at[others], tile_recv_sems.at[part])

        def widen_samples(source, carry):
            samples[source] = tiles_in[tile_rows(part * sources + source), :].astype(F32)
            return carry

        lax.fori_loop(0, sources, widen_samples, 0)

    count_x = NXI // HALVES
    group_rows = 2 * GC * WY

    def grid_part(part, groups):
        def one_side(side, carry):
            step = side * KP + part

            def weigh(source, carry):
                at = pl.ds(pl.multiple_of((step * bins + source) * WY, WY), WY)
                real, imag = row_real[at, :], row_imag[at, :]
                lanes = pl.ds(pl.multiple_of(source * LANES, LANES), LANES)
                for at_group, group in enumerate(groups):
                    for coil in range(GC):
                        row = group * GC + coil
                        data_real = samples[side * bins + source, row : row + 1, :]
                        data_imag = samples[side * bins + source, row + C : row + C + 1, :]
                        first = at_group * group_rows + coil * WY
                        weighted[first : first + WY, lanes] = (
                            real * data_real - imag * data_imag
                        ).astype(BF16)
                        first = first + GC * WY
                        weighted[first : first + WY, lanes] = (
                            real * data_imag + imag * data_real
                        ).astype(BF16)
                return carry

            lax.fori_loop(0, bins, weigh, 0)
            products[: len(groups) * group_rows, :] = jnp.dot(
                weighted[: len(groups) * group_rows, :],
                kernel_x[step],
                preferred_element_type=F32,
            )
            shape = (half_slabs, rows // 2, LANES)
            at = pl.ds(pl.multiple_of(step * rows, rows), rows)
            for at_group, group in enumerate(groups):
                first = at_group * group_rows
                above_rows = slice(first, first + group_rows // 2)
                below_rows = slice(first + group_rows // 2, first + group_rows)
                real = products[above_rows, :count_x] - products[below_rows, count_x:]
                imag = products[below_rows, :count_x] + products[above_rows, count_x:]
                spectra = jnp.concatenate([real.T.reshape(shape), imag.T.reshape(shape)], axis=1)
                sending[group, :, at, :] = spectra.astype(BF16)
            return carry

        lax.fori_loop(0, HALVES, one_side, 0)

    for part in range(KP - 1):
        take_tiles(part)
        grid_part(part, tuple(range(COIL_GROUPS)))
    take_tiles(KP - 1)
    for group in range(COIL_GROUPS):
        grid_part(KP - 1, (group,))
        for step in range(1, half_slabs):
            peer = half_peer(step)
            pltpu.make_async_remote_copy(
                sending.at[group, peer],
                received.at[group, place],
                group_send_sems.at[group],
                group_recv_sems.at[group],
                {"slab": half * half_slabs + peer},
                MESH,
            ).start()
        own_copy(group).start()

    loads[8].wait()
    loads[9].wait()
    features = GC * WY
    for group in range(COIL_GROUPS):
        own_copy(group).wait()
        others = pl.ds(0, half_slabs - 1)
        all_bytes(received.at[group, others], group_recv_sems.at[group])

        def widen(source, carry, group=group):
            at = pl.ds(source * parts, parts)
            widened[at] = received[group, source].astype(F32).reshape(parts, rows, LANES)
            return carry

        lax.fori_loop(0, half_slabs, widen, 0)
        for pair in range(rows // 4):
            inputs = []
            for at_x in (2 * pair, 2 * pair + 1):
                real = widened[:, at_x, :].astype(BF16)
                imag = widened[:, rows // 2 + at_x, :].astype(BF16)
                inputs.append(jnp.concatenate([real, imag], axis=0))
            images = jnp.dot(
                z_table[...], jnp.concatenate(inputs, axis=1), preferred_element_type=F32
            )
            for at, at_x in enumerate((2 * pair, 2 * pair + 1)):
                image_real = images[:depth, at * LANES : (at + 1) * LANES]
                image_imag = images[depth:, at * LANES : (at + 1) * LANES]
                first = 2 * at_x * C * WY + group * features
                sens_real = sens[:, first : first + features].astype(F32)
                first = first + C * WY
                sens_imag = sens[:, first : first + features].astype(F32)
                real = sens_real * image_real + sens_imag * image_imag
                imag = sens_real * image_imag - sens_imag * image_real
                if group > 0:
                    real = real + total[2 * at_x]
                    imag = imag + total[2 * at_x + 1]
                total[2 * at_x] = real
                total[2 * at_x + 1] = imag

    others = pl.ds(0, half_slabs - 1)
    for group in range(COIL_GROUPS):
        all_bytes(sending.at[group, others], group_send_sems.at[group])
    all_bytes(coords_in.at[pl.ds(0, (sources - 1) * 8)], send_sems.at[0])
    for part in range(KP):
        all_bytes(tiles_in.at[tile_rows(0, sources - 1)], tile_send_sems.at[part])

    @pl.when(jnp.logical_not(is_first))
    def _():
        image_copy.wait_send()
        edge_copy.wait_recv()

    @pl.when(jnp.logical_not(is_last))
    def _():
        edge_copy.wait_send()

    scaling = 1.0 / math.sqrt(P_SIZE * bins * BLKB * depth * C / KP)
    for part in range(rows // 8):
        lanes = slice(part * LANES, (part + 1) * LANES)
        value = jnp.concatenate([total[part * 8 + at] for at in range(8)], axis=1)
        high = value.astype(BF16)
        low = (value - high.astype(F32)).astype(BF16)
        line = jnp.dot(high, fold[...], preferred_element_type=F32)
        line = line + jnp.dot(low, fold[...], preferred_element_type=F32)
        out_ref[:, lanes] = below[:, lanes] - own_edge[:, lanes] - line * scaling


def slab_gradient(
    bins, slabs, data, route, spoke, segment, count, sens, image, weight, x_table, z_table
):
    hbm = pl.BlockSpec(memory_space=pltpu.HBM)
    depth = sens.shape[0]
    blocks = data.shape[0]
    rows = 2 * NXI // slabs
    sources = HALVES * bins
    parts = HALVES * KP
    half_slabs = slabs // HALVES
    operands = (data, route, spoke, segment, count, sens, image, weight, x_table, z_table)
    held = operands[:8] + (x_table[0], z_table)
    return pl.pallas_call(
        functools.partial(slab_kernel, bins, slabs),
        out_shape=jax.ShapeDtypeStruct(image.shape, F32),
        in_specs=[hbm] * len(operands),
        out_specs=pl.BlockSpec(memory_space=pltpu.VMEM),
        scratch_shapes=[pltpu.VMEM(array.shape, array.dtype) for array in held]
        + [
            pltpu.VMEM((4 * blocks, 4 * LANES), BF16),
            pltpu.VMEM((bins * KP * 16, 4 * LANES), F32),
            pltpu.VMEM((bins * ROUTE_ROWS, LANES), BF16),
            pltpu.VMEM((bins * 8, LANES), F32),
            pltpu.VMEM((sources * ROUTE_ROWS, LANES), BF16),
            pltpu.VMEM((sources * 8, LANES), F32),
            pltpu.VMEM(image.shape, F32),
            pltpu.VMEM(image.shape, F32),
            pltpu.VMEM(image.shape, F32),
            pltpu.VMEM((sources, PC, LANES), F32),
            pltpu.VMEM((parts * bins * WY, LANES), F32),
            pltpu.VMEM((parts * bins * WY, LANES), F32),
            pltpu.VMEM((bins * LANES, NG), BF16),
            pltpu.VMEM((parts, bins * LANES, 2 * NXI // HALVES), BF16),
            pltpu.VMEM((2 * C * WY, bins * LANES), BF16),
            pltpu.VMEM((2 * C * WY, 2 * NXI // HALVES), F32),
            pltpu.VMEM((COIL_GROUPS, half_slabs, parts * rows, LANES), BF16),
            pltpu.VMEM((COIL_GROUPS, half_slabs, parts * rows, LANES), BF16),
            pltpu.VMEM((depth, rows, LANES), F32),
            pltpu.VMEM((rows, depth, LANES), F32),
            pltpu.VMEM((8 * LANES, LANES), BF16),
            pltpu.SemaphoreType.DMA((len(operands),)),
            pltpu.SemaphoreType.DMA((1 + KP + COIL_GROUPS,)),
            pltpu.SemaphoreType.DMA((3,)),
            pltpu.SemaphoreType.DMA((3,)),
            pltpu.SemaphoreType.DMA((KP,)),
            pltpu.SemaphoreType.DMA((KP,)),
            pltpu.SemaphoreType.DMA((COIL_GROUPS,)),
            pltpu.SemaphoreType.DMA((COIL_GROUPS,)),
        ],
        compiler_params=pltpu.CompilerParams(
            collective_id=0, has_side_effects=True, vmem_limit_bytes=60 << 20
        ),
    )(*operands)


def waves(out_index, in_index, modulus):
    angles = 2.0 * math.pi / modulus * (out_index[:, None] * in_index[None, :] % modulus)
    return np.cos(angles), np.sin(angles)


def x_phases():
    cosine, sine = waves(np.arange(NXI) - NXI // 2, np.arange(NG) - NG // 2, NG)
    shape = (HALVES, NXI // HALVES, NG)
    table = np.concatenate([cosine.reshape(shape), sine.reshape(shape)], axis=1)
    return table.transpose(0, 2, 1)


def z_phases(slabs):
    depth = KP * slabs
    order = np.arange(depth).reshape(HALVES, slabs // HALVES, KP).transpose(1, 0, 2).reshape(-1)
    cosine, sine = waves(np.arange(depth) - depth // 2, order - depth // 2, depth)
    return np.concatenate(
        [np.concatenate([cosine, -sine], axis=1), np.concatenate([sine, cosine], axis=1)], axis=0
    )


def shards(
    sample_data,
    block_route,
    spoke_index,
    segment_index,
    sample_count,
    sensitivity,
    image,
    tv_weight,
):
    bins = lax.axis_size("bin")
    slabs = lax.axis_size("slab")
    gradient = slab_gradient(
        bins,
        slabs,
        sample_data,
        block_route.reshape(1, -1),
        spoke_index.reshape(1, -1),
        segment_index.reshape(1, -1),
        sample_count.reshape(1, -1),
        sensitivity,
        image[0],
        tv_weight[0],
        jnp.asarray(x_phases().astype(ml_dtypes.bfloat16)),
        jnp.asarray(z_phases(slabs).astype(ml_dtypes.bfloat16)),
    )
    return gradient.reshape(image.shape)


def solution(mesh):
    return jax.shard_map(
        shards,
        mesh=mesh,
        in_specs=(
            P(("bin", "slab"), None),
            P(("bin", "slab"), None),
            P(("bin", "slab")),
            P(("bin", "slab")),
            P(("bin", "slab")),
            P(None, "slab"),
            P("bin", None, "slab"),
            P("bin", None, "slab"),
        ),
        out_specs=P("bin", None, "slab"),
        check_vma=False,
    )
```

```python
import functools
import math

import jax
import jax.numpy as jnp
import ml_dtypes
import numpy as np
from jax import lax
from jax.experimental import pallas as pl
from jax.experimental.pallas import tpu as pltpu
from jax.sharding import PartitionSpec as P

C = 32
NG = 384
NXI = 256
WY = 16
RO = 384
P_SIZE = 32
KP = 3
BLKB = 4
CAPK = 4

SMOOTHING = 0.5
GOLDEN_STEP = 40503
TURN_STEPS = 65536

F32 = jnp.float32
BF16 = jnp.bfloat16
LANES = 128
PC = 2 * C
ROUTE_ROWS = KP * PC
HALVES = 2
COIL_GROUPS = 4
GC = C // COIL_GROUPS
MESH = pl.DeviceIdType.MESH
FAR = -1000.0


def iota(shape, dim):
    return lax.broadcasted_iota(jnp.int32, shape, dim)


def turn_waves(turns):
    quarter = jnp.floor(4.0 * turns + 0.5)
    angle = (2.0 * math.pi) * (turns - 0.25 * quarter)
    sq = angle * angle
    sine = angle + angle * sq * (
        -1.0 / 6 + sq * (1.0 / 120 + sq * (-1.0 / 5040 + sq * (1.0 / 362880)))
    )
    cosine = 1.0 + sq * (
        -0.5 + sq * (1.0 / 24 + sq * (-1.0 / 720 + sq * (1.0 / 40320 + sq * (-1.0 / 3628800))))
    )
    turn = quarter - 4.0 * jnp.floor(0.25 * quarter)
    odd = (turn == 1.0) | (turn == 3.0)
    first = jnp.where(odd, sine, cosine)
    second = jnp.where(odd, cosine, sine)
    cos_out = jnp.where((turn == 1.0) | (turn == 2.0), -first, first)
    sin_out = jnp.where(turn >= 2.0, -second, second)
    return cos_out, sin_out


def tap_weights(coord):
    cell = jnp.floor(coord)
    ahead = coord - cell
    behind = 1.0 - ahead
    return cell, [
        behind * behind * behind * (1.0 / 6.0),
        2.0 / 3.0 + ahead * ahead * (0.5 * ahead - 1.0),
        2.0 / 3.0 + behind * behind * (0.5 * behind - 1.0),
        ahead * ahead * ahead * (1.0 / 6.0),
    ]


def all_bytes(ref, sem):
    pltpu.make_async_copy(ref, ref, sem).wait()


def slab_kernel(
    bins,
    slabs,
    data_hbm,
    route_hbm,
    spoke_hbm,
    segment_hbm,
    count_hbm,
    sens_hbm,
    image_hbm,
    weight_hbm,
    x_table_hbm,
    z_table_hbm,
    out_ref,
    data,
    route,
    spoke,
    segment,
    count,
    sens,
    image,
    weight,
    x_table,
    z_table,
    stacked,
    placed_rows,
    tiles,
    coords,
    tiles_in,
    coords_in,
    above,
    below,
    own_edge,
    samples,
    row_real,
    row_imag,
    across,
    kernel_x,
    weighted,
    products,
    sending,
    received,
    widened,
    total,
    fold,
    load_sems,
    own_sems,
    send_sems,
    recv_sems,
    tile_send_sems,
    tile_recv_sems,
    group_send_sems,
    group_recv_sems,
):
    slab = lax.axis_index("slab")
    me = lax.axis_index("bin")
    half_slabs = slabs // HALVES
    half = lax.div(slab, half_slabs)
    place = lax.rem(slab, half_slabs)
    opposite = lax.rem(slab + half_slabs, slabs)
    sources = HALVES * bins
    parts = HALVES * KP
    depth = KP * slabs
    rows = 2 * NXI // slabs
    wide = out_ref.shape[1]
    blocks = data.shape[0]

    barrier = pltpu.get_barrier_semaphore()
    route_peers = [(side, step) for side in (0, 1) for step in (4, 5, 3, 6, 7, 1, 2, 0)]
    route_peers.remove((0, 0))

    def route_peer(across_half, step):
        return {
            "bin": lax.rem(me + step, bins),
            "slab": opposite if across_half else slab,
        }

    half_order = [(dz, dy, dc) for dz in (0, 1) for dy in (2, 1, 3) for dc in (0, 1)]
    half_order += [(1, 0, 0), (1, 0, 1), (0, 0, 1)]

    def half_peer(dz, dy, dc):
        z, y, core = lax.div(place, 8), lax.rem(lax.div(place, 2), 4), lax.rem(place, 2)
        return 8 * lax.rem(z + dz, 2) + 2 * lax.rem(y + dy, 4) + lax.rem(core + dc, 2)

    for pair in route_peers:
        pl.semaphore_signal(barrier, inc=1, device_id=route_peer(*pair), device_id_type=MESH)
    for hop in half_order:
        pl.semaphore_signal(
            barrier,
            inc=1,
            device_id={"slab": half * half_slabs + half_peer(*hop)},
            device_id_type=MESH,
        )

    loads = [
        pltpu.make_async_copy(from_ref, to_ref, load_sems.at[at])
        for at, (from_ref, to_ref) in enumerate(
            [
                (route_hbm, route),
                (spoke_hbm, spoke),
                (segment_hbm, segment),
                (count_hbm, count),
                (data_hbm, data),
                (image_hbm, image),
                (weight_hbm, weight),
                (x_table_hbm.at[half], x_table),
                (z_table_hbm, z_table),
                (sens_hbm, sens),
            ]
        )
    ]
    for copy in loads:
        copy.start()
    for copy in loads[:4]:
        copy.wait()

    row = iota((blocks, LANES), 0)
    lane = iota((blocks, LANES), 1)
    lane_block = lane & (blocks - 1)

    def column(ref_row):
        spread = jnp.broadcast_to(ref_row.astype(F32), (blocks, blocks))
        eye = iota((blocks, blocks), 0) == iota((blocks, blocks), 1)
        return jnp.sum(jnp.where(eye, spread, 0.0), axis=1, keepdims=True)

    route_col = jnp.broadcast_to(column(route[...]), (blocks, LANES))
    route_row = jnp.sum(jnp.where(row == lane_block, route_col, 0.0), axis=0, keepdims=True)
    same = route_col == jnp.broadcast_to(route_row, (blocks, LANES))
    rank_row = jnp.sum(jnp.where(same & (row < lane_block), 1.0, 0.0), axis=0, keepdims=True)
    rank_col = jnp.sum(jnp.where(same & (lane < row), 1.0, 0.0), axis=1, keepdims=True)
    slot_row = route_row * CAPK + rank_row

    turn_row = (spoke[...] * GOLDEN_STEP) & (TURN_STEPS - 1)
    columns = [column(turn_row >> 8), column(turn_row & 255), column(segment[...]), column(count[...])]
    slot_hit = rank_col == (lane & (CAPK - 1)).astype(F32)
    picks = [jnp.where(slot_hit, value, 0.0) for value in columns]
    picks = jnp.concatenate(picks, axis=1).astype(BF16)
    picks = jnp.concatenate(
        [picks, jnp.zeros((LANES - blocks, len(columns) * LANES), BF16)], axis=0
    )
    coord_shape = (8 * bins, LANES)
    out_row = iota(coord_shape, 0)
    out_lane = iota(coord_shape, 1)
    part_row = out_row & 7
    is_x = part_row < KP
    partition = jnp.where(is_x, part_row, part_row - KP)
    row_route = jnp.where(part_row < 2 * KP, KP * (out_row >> 3) + partition, -1).astype(F32)
    chosen = (row_route == jnp.broadcast_to(route_row, coord_shape)) & (out_lane < blocks)
    spread = jnp.dot(jnp.where(chosen, 1.0, 0.0).astype(BF16), picks, preferred_element_type=F32)
    turns = (256.0 * spread[:, :LANES] + spread[:, LANES : 2 * LANES]) * (1.0 / TURN_STEPS)
    cosine, sine = turn_waves(turns)
    sample = (2 * ((out_lane & 63) >> 2) + (out_lane >> 6)).astype(F32)
    radial = (P_SIZE * spread[:, 2 * LANES : 3 * LANES] + sample - RO // 2 + 0.5) * ((NG - 8) / RO)
    coord_x = jnp.where(sample < spread[:, 3 * LANES :], NG / 2 + radial * cosine, FAR)
    coord_y = NG / 2 + radial * sine
    coords[...] = jnp.where(is_x, coord_x, coord_y)

    def coord_rows(index):
        return pl.ds(pl.multiple_of(index * 8, 8), 8)

    def tile_rows(index, many=1):
        return pl.ds(pl.multiple_of(index * PC, PC), many * PC)

    my_source = half * bins + me
    image_copy = pltpu.make_async_remote_copy(
        image,
        above,
        send_sems.at[1],
        recv_sems.at[1],
        {"bin": lax.rem(me + bins - 1, bins)},
        MESH,
    )
    edge_copy = pltpu.make_async_remote_copy(
        own_edge, below, send_sems.at[2], recv_sems.at[2], {"bin": lax.rem(me + 1, bins)}, MESH
    )
    is_first = me == 0
    is_last = me == bins - 1
    loads[5].wait()
    pl.semaphore_wait(barrier, len(route_peers) + half_slabs - 1)

    @pl.when(jnp.logical_not(is_first))
    def _():
        image_copy.start()

    for pair in route_peers:
        peer = route_peer(*pair)
        pltpu.make_async_remote_copy(
            coords.at[coord_rows(peer["bin"])],
            coords_in.at[coord_rows(my_source)],
            send_sems.at[0],
            recv_sems.at[0],
            peer,
            MESH,
        ).start()
    own_coords = pltpu.make_async_copy(
        coords.at[coord_rows(me)], coords_in.at[coord_rows(my_source)], own_sems.at[0]
    )
    own_coords.start()

    loads[4].wait()
    big = (bins * KP * 16, LANES)
    place_row = iota(big, 0)
    place_lane = iota(big, 1)
    wanted = (CAPK * (place_row >> 4) + (place_row & 3)).astype(F32)
    hit = (wanted == jnp.broadcast_to(slot_row, big)) & (((place_row >> 2) & 3) == (place_lane >> 5))
    one_hot = jnp.where(hit, 1.0, 0.0).astype(BF16)
    for quarter in range(4):
        for fourth in range(4):
            first = (4 * fourth + quarter) * LANES
            to_rows = slice(quarter * blocks, (quarter + 1) * blocks)
            stacked[to_rows, fourth * LANES : (fourth + 1) * LANES] = data[:, first : first + LANES]
    placed_rows[...] = jnp.dot(one_hot, stacked[...], preferred_element_type=F32)
    half_lane = iota((PC, LANES), 1) < 64

    def turn_pair(pair, carry):
        base = pl.multiple_of(pair * 32, 32)
        pieces = [
            placed_rows[pl.ds(base + 16 * one, 16), fourth * LANES : (fourth + 1) * LANES]
            for one in range(2)
            for fourth in range(4)
        ]
        turned = jnp.concatenate(pieces, axis=0).T
        low, high = turned[:PC], turned[PC:]
        at = pl.multiple_of(pair * 2 * PC, 2 * PC)
        tiles[pl.ds(at, PC), :] = jnp.where(half_lane, low, pltpu.roll(high, 64, 1)).astype(BF16)
        tiles[pl.ds(at + PC, PC), :] = jnp.where(half_lane, pltpu.roll(low, 64, 1), high).astype(BF16)
        return carry

    lax.fori_loop(0, bins * KP // 2, turn_pair, 0)
    own_tiles = []
    for part in range(KP):
        slot = part * sources + my_source
        for pair in route_peers:
            peer = route_peer(*pair)
            pltpu.make_async_remote_copy(
                tiles.at[tile_rows(peer["bin"] * KP + part)],
                tiles_in.at[tile_rows(slot)],
                tile_send_sems.at[part],
                tile_recv_sems.at[part],
                peer,
                MESH,
            ).start()
        copy = pltpu.make_async_copy(
            tiles.at[tile_rows(me * KP + part)], tiles_in.at[tile_rows(slot)], own_sems.at[1 + part]
        )
        copy.start()
        own_tiles.append(copy)

    fold_row = iota(fold.shape, 0)
    fold_lane = iota(fold.shape, 1)
    folds = ((fold_lane >> 4) == (fold_row >> 7)) & ((fold_lane & 15) == (fold_row & 15))
    fold[...] = jnp.where(folds, 1.0, 0.0).astype(BF16)

    own_coords.wait()
    others = pl.ds(0, (sources - 1) * 8)
    all_bytes(coords_in.at[others], recv_sems.at[0])
    loads[7].wait()
    y_offset = (iota((WY, LANES), 0) - WY // 2).astype(F32)
    taps = [turn_waves(y_offset * (m / NG)) for m in range(1, 4)]

    def prepare(step, carry):
        side = lax.div(step, KP)
        part = lax.rem(step, KP)

        def prepare_source(source, carry):
            base = pl.multiple_of((side * bins + source) * 8, 8)
            coord_x = coords_in[pl.ds(base + part, 1), :]
            coord_y = coords_in[pl.ds(base + KP + part, 1), :]
            cell, weights = tap_weights(coord_y)
            steps = y_offset * (cell - (1.0 + NG // 2))
            base_turns = steps * (1.0 / NG)
            base_cos, base_sin = turn_waves(base_turns - jnp.floor(base_turns))
            sum_cos = jnp.broadcast_to(weights[0], (WY, LANES))
            sum_sin = jnp.zeros((WY, LANES), F32)
            for tap_weight, (tap_cos, tap_sin) in zip(weights[1:], taps):
                sum_cos = sum_cos + tap_weight * tap_cos
                sum_sin = sum_sin + tap_weight * tap_sin
            at = pl.ds(pl.multiple_of((step * bins + source) * WY, WY), WY)
            row_real[at, :] = sum_cos * base_cos - sum_sin * base_sin
            row_imag[at, :] = sum_cos * base_sin + sum_sin * base_cos
            lanes = pl.ds(pl.multiple_of(source * LANES, LANES), LANES)
            cell, weights = tap_weights(coord_x)
            tile = (16, LANES)
            weights = [jnp.broadcast_to(tap, tile).astype(BF16) for tap in weights]
            for block in range(0, NG, LANES):
                start = jnp.clip(cell - (1.0 + block), -8.0, LANES + 8.0)
                away = (iota(tile, 0).astype(F32) - start).astype(BF16)
                for first in range(0, LANES, tile[0]):
                    value = jnp.zeros(tile, BF16)
                    for tap, tap_weight in enumerate(weights):
                        value = jnp.where(away == jnp.array(tap - first, BF16), tap_weight, value)
                    across[block + first : block + first + tile[0], lanes] = value
            return carry

        lax.fori_loop(0, bins, prepare_source, 0)
        kernel_x[step] = lax.dot_general(
            across[...], x_table[...], (((0,), (0,)), ((), ())), preferred_element_type=F32
        ).astype(BF16)
        return carry

    lax.fori_loop(0, parts, prepare, 0)

    loads[6].wait()

    @pl.when(jnp.logical_not(is_last))
    def _():
        image_copy.wait_recv()

    @pl.when(is_last)
    def _():
        above[...] = image[...]

    lane = iota((depth, wide), 1)
    upper_half = ((lane >> 4) & 1) == 1
    from_lane = iota((wide // 2, wide), 0)
    to_lane = iota((wide // 2, wide), 1)
    widen_weight = jnp.where(from_lane == ((to_lane >> 5) << 4) + (to_lane & 15), 1.0, 0.0)
    difference = above[...] - image[...]
    square = difference * difference
    other = jnp.where(upper_half, pltpu.roll(square, 16, 1), pltpu.roll(square, wide - 16, 1))
    magnitude = jnp.sqrt(square + other + SMOOTHING * SMOOTHING)
    wide_weight = jnp.dot(
        weight[...], widen_weight, preferred_element_type=F32, precision=lax.Precision.HIGHEST
    )
    own_edge[...] = wide_weight * difference / magnitude

    @pl.when(jnp.logical_not(is_last))
    def _():
        edge_copy.start()

    @pl.when(is_first)
    def _():
        below[...] = jnp.zeros_like(below)

    def own_copy(group):
        return pltpu.make_async_copy(
            sending.at[group, place], received.at[group, place], own_sems.at[1 + KP + group]
        )

    def take_tiles(part):
        own_tiles[part].wait()
        others = tile_rows(part * sources, sources - 1)
        all_bytes(tiles_in.at[others], tile_recv_sems.at[part])

        def widen_samples(source, carry):
            slot = part * sources + source
            samples[slot] = tiles_in[tile_rows(slot), :].astype(F32)
            return carry

        lax.fori_loop(0, sources, widen_samples, 0)

    count_x = NXI // HALVES
    group_rows = 2 * GC * WY

    def grid_part(part, groups):
        def one_side(side, carry):
            step = side * KP + part

            def weigh(source, carry):
                at = pl.ds(pl.multiple_of((step * bins + source) * WY, WY), WY)
                real, imag = row_real[at, :], row_imag[at, :]
                lanes = pl.ds(pl.multiple_of(source * LANES, LANES), LANES)
                for at_group, group in enumerate(groups):
                    for coil in range(GC):
                        row = group * GC + coil
                        data_real = samples[part * sources + side * bins + source, row : row + 1, :]
                        data_imag = samples[part * sources + side * bins + source, row + C : row + C + 1, :]
                        first = at_group * group_rows + coil * WY
                        weighted[first : first + WY, lanes] = (
                            real * data_real - imag * data_imag
                        ).astype(BF16)
                        first = first + GC * WY
                        weighted[first : first + WY, lanes] = (
                            real * data_imag + imag * data_real
                        ).astype(BF16)
                return carry

            lax.fori_loop(0, bins, weigh, 0)
            products[: len(groups) * group_rows, :] = jnp.dot(
                weighted[: len(groups) * group_rows, :],
                kernel_x[step],
                preferred_element_type=F32,
            )
            shape = (half_slabs, rows // 2, LANES)
            at = pl.ds(pl.multiple_of(step * rows, rows), rows)
            for at_group, group in enumerate(groups):
                first = at_group * group_rows
                above_rows = slice(first, first + group_rows // 2)
                below_rows = slice(first + group_rows // 2, first + group_rows)
                real = products[above_rows, :count_x] - products[below_rows, count_x:]
                imag = products[below_rows, :count_x] + products[above_rows, count_x:]
                spectra = jnp.concatenate([real.T.reshape(shape), imag.T.reshape(shape)], axis=1)
                sending[group, :, at, :] = spectra.astype(BF16)
            return carry

        lax.fori_loop(0, HALVES, one_side, 0)

    def send_group(group):
        for hop in half_order:
            peer = half_peer(*hop)
            pltpu.make_async_remote_copy(
                sending.at[group, peer],
                received.at[group, place],
                group_send_sems.at[group],
                group_recv_sems.at[group],
                {"slab": half * half_slabs + peer},
                MESH,
            ).start()
        own_copy(group).start()

    early = tuple(range(COIL_GROUPS // 2))
    late = tuple(range(COIL_GROUPS // 2, COIL_GROUPS))
    for part in range(KP - 1):
        take_tiles(part)
        grid_part(part, early)
    take_tiles(KP - 1)
    for group in early:
        grid_part(KP - 1, (group,))
        send_group(group)
    for part in range(KP):
        grid_part(part, late)
    for group in late:
        send_group(group)

    loads[8].wait()
    loads[9].wait()
    features = GC * WY
    for group in range(COIL_GROUPS):
        own_copy(group).wait()
        others = pl.ds(0, half_slabs - 1)
        all_bytes(received.at[group, others], group_recv_sems.at[group])

        def widen(source, carry, group=group):
            at = pl.ds(source * parts, parts)
            widened[at] = received[group, source].astype(F32).reshape(parts, rows, LANES)
            return carry

        lax.fori_loop(0, half_slabs, widen, 0)
        for pair in range(rows // 4):
            inputs = []
            for at_x in (2 * pair, 2 * pair + 1):
                real = widened[:, at_x, :].astype(BF16)
                imag = widened[:, rows // 2 + at_x, :].astype(BF16)
                inputs.append(jnp.concatenate([real, imag], axis=0))
            images = jnp.dot(
                z_table[...], jnp.concatenate(inputs, axis=1), preferred_element_type=F32
            )
            for at, at_x in enumerate((2 * pair, 2 * pair + 1)):
                image_real = images[:depth, at * LANES : (at + 1) * LANES]
                image_imag = images[depth:, at * LANES : (at + 1) * LANES]
                first = 2 * at_x * C * WY + group * features
                sens_real = sens[:, first : first + features].astype(F32)
                first = first + C * WY
                sens_imag = sens[:, first : first + features].astype(F32)
                real = sens_real * image_real + sens_imag * image_imag
                imag = sens_real * image_imag - sens_imag * image_real
                if group > 0:
                    real = real + total[2 * at_x]
                    imag = imag + total[2 * at_x + 1]
                total[2 * at_x] = real
                total[2 * at_x + 1] = imag

    others = pl.ds(0, half_slabs - 1)
    for group in range(COIL_GROUPS):
        all_bytes(sending.at[group, others], group_send_sems.at[group])
    all_bytes(coords_in.at[pl.ds(0, (sources - 1) * 8)], send_sems.at[0])
    for part in range(KP):
        all_bytes(tiles_in.at[tile_rows(0, sources - 1)], tile_send_sems.at[part])

    @pl.when(jnp.logical_not(is_first))
    def _():
        image_copy.wait_send()
        edge_copy.wait_recv()

    @pl.when(jnp.logical_not(is_last))
    def _():
        edge_copy.wait_send()

    scaling = 1.0 / math.sqrt(P_SIZE * bins * BLKB * depth * C / KP)
    for part in range(rows // 8):
        lanes = slice(part * LANES, (part + 1) * LANES)
        value = jnp.concatenate([total[part * 8 + at] for at in range(8)], axis=1)
        high = value.astype(BF16)
        low = (value - high.astype(F32)).astype(BF16)
        line = jnp.dot(high, fold[...], preferred_element_type=F32)
        line = line + jnp.dot(low, fold[...], preferred_element_type=F32)
        out_ref[:, lanes] = below[:, lanes] - own_edge[:, lanes] - line * scaling


def slab_gradient(
    bins, slabs, data, route, spoke, segment, count, sens, image, weight, x_table, z_table
):
    hbm = pl.BlockSpec(memory_space=pltpu.HBM)
    depth = sens.shape[0]
    blocks = data.shape[0]
    rows = 2 * NXI // slabs
    sources = HALVES * bins
    parts = HALVES * KP
    half_slabs = slabs // HALVES
    operands = (data, route, spoke, segment, count, sens, image, weight, x_table, z_table)
    held = operands[:8] + (x_table[0], z_table)
    return pl.pallas_call(
        functools.partial(slab_kernel, bins, slabs),
        out_shape=jax.ShapeDtypeStruct(image.shape, F32),
        in_specs=[hbm] * len(operands),
        out_specs=pl.BlockSpec(memory_space=pltpu.VMEM),
        scratch_shapes=[pltpu.VMEM(array.shape, array.dtype) for array in held]
        + [
            pltpu.VMEM((4 * blocks, 4 * LANES), BF16),
            pltpu.VMEM((bins * KP * 16, 4 * LANES), F32),
            pltpu.VMEM((bins * ROUTE_ROWS, LANES), BF16),
            pltpu.VMEM((bins * 8, LANES), F32),
            pltpu.VMEM((sources * ROUTE_ROWS, LANES), BF16),
            pltpu.VMEM((sources * 8, LANES), F32),
            pltpu.VMEM(image.shape, F32),
            pltpu.VMEM(image.shape, F32),
            pltpu.VMEM(image.shape, F32),
            pltpu.VMEM((KP * sources, PC, LANES), F32),
            pltpu.VMEM((parts * bins * WY, LANES), F32),
            pltpu.VMEM((parts * bins * WY, LANES), F32),
            pltpu.VMEM((NG, bins * LANES), BF16),
            pltpu.VMEM((parts, bins * LANES, 2 * NXI // HALVES), BF16),
            pltpu.VMEM((2 * C * WY, bins * LANES), BF16),
            pltpu.VMEM((2 * C * WY, 2 * NXI // HALVES), F32),
            pltpu.VMEM((COIL_GROUPS, half_slabs, parts * rows, LANES), BF16),
            pltpu.VMEM((COIL_GROUPS, half_slabs, parts * rows, LANES), BF16),
            pltpu.VMEM((depth, rows, LANES), F32),
            pltpu.VMEM((rows, depth, LANES), F32),
            pltpu.VMEM((8 * LANES, LANES), BF16),
            pltpu.SemaphoreType.DMA((len(operands),)),
            pltpu.SemaphoreType.DMA((1 + KP + COIL_GROUPS,)),
            pltpu.SemaphoreType.DMA((3,)),
            pltpu.SemaphoreType.DMA((3,)),
            pltpu.SemaphoreType.DMA((KP,)),
            pltpu.SemaphoreType.DMA((KP,)),
            pltpu.SemaphoreType.DMA((COIL_GROUPS,)),
            pltpu.SemaphoreType.DMA((COIL_GROUPS,)),
        ],
        compiler_params=pltpu.CompilerParams(
            collective_id=0, has_side_effects=True, vmem_limit_bytes=60 << 20
        ),
    )(*operands)


def waves(out_index, in_index, modulus):
    angles = 2.0 * math.pi / modulus * (out_index[:, None] * in_index[None, :] % modulus)
    return np.cos(angles), np.sin(angles)


def x_phases():
    cosine, sine = waves(np.arange(NXI) - NXI // 2, np.arange(NG) - NG // 2, NG)
    shape = (HALVES, NXI // HALVES, NG)
    table = np.concatenate([cosine.reshape(shape), sine.reshape(shape)], axis=1)
    return table.transpose(0, 2, 1)


def z_phases(slabs):
    depth = KP * slabs
    order = np.arange(depth).reshape(HALVES, slabs // HALVES, KP).transpose(1, 0, 2).reshape(-1)
    cosine, sine = waves(np.arange(depth) - depth // 2, order - depth // 2, depth)
    return np.concatenate(
        [np.concatenate([cosine, -sine], axis=1), np.concatenate([sine, cosine], axis=1)], axis=0
    )


def shards(
    sample_data,
    block_route,
    spoke_index,
    segment_index,
    sample_count,
    sensitivity,
    image,
    tv_weight,
):
    bins = lax.axis_size("bin")
    slabs = lax.axis_size("slab")
    gradient = slab_gradient(
        bins,
        slabs,
        sample_data,
        block_route.reshape(1, -1),
        spoke_index.reshape(1, -1),
        segment_index.reshape(1, -1),
        sample_count.reshape(1, -1),
        sensitivity,
        image[0],
        tv_weight[0],
        jnp.asarray(x_phases().astype(ml_dtypes.bfloat16)),
        jnp.asarray(z_phases(slabs).astype(ml_dtypes.bfloat16)),
    )
    return gradient.reshape(image.shape)


def solution(mesh):
    return jax.shard_map(
        shards,
        mesh=mesh,
        in_specs=(
            P(("bin", "slab"), None),
            P(("bin", "slab"), None),
            P(("bin", "slab")),
            P(("bin", "slab")),
            P(("bin", "slab")),
            P(None, "slab"),
            P("bin", None, "slab"),
            P("bin", None, "slab"),
        ),
        out_specs=P("bin", None, "slab"),
        check_vma=False,
    )
```

```python
import functools
import math

import jax
import jax.numpy as jnp
import ml_dtypes
import numpy as np
from jax import lax
from jax.experimental import pallas as pl
from jax.experimental.pallas import tpu as pltpu
from jax.sharding import PartitionSpec as P

C = 32
NG = 384
NXI = 256
WY = 16
RO = 384
P_SIZE = 32
KP = 3
BLKB = 4
CAPK = 4

SMOOTHING = 0.5
GOLDEN_STEP = 40503
TURN_STEPS = 65536

F32 = jnp.float32
BF16 = jnp.bfloat16
LANES = 128
PC = 2 * C
ROUTE_ROWS = KP * PC
HALVES = 2
COIL_GROUPS = 4
GC = C // COIL_GROUPS
MESH = pl.DeviceIdType.MESH
FAR = -1000.0


def iota(shape, dim):
    return lax.broadcasted_iota(jnp.int32, shape, dim)


def turn_waves(turns):
    quarter = jnp.floor(4.0 * turns + 0.5)
    angle = (2.0 * math.pi) * (turns - 0.25 * quarter)
    sq = angle * angle
    sine = angle + angle * sq * (
        -1.0 / 6 + sq * (1.0 / 120 + sq * (-1.0 / 5040 + sq * (1.0 / 362880)))
    )
    cosine = 1.0 + sq * (
        -0.5 + sq * (1.0 / 24 + sq * (-1.0 / 720 + sq * (1.0 / 40320 + sq * (-1.0 / 3628800))))
    )
    turn = quarter - 4.0 * jnp.floor(0.25 * quarter)
    odd = (turn == 1.0) | (turn == 3.0)
    first = jnp.where(odd, sine, cosine)
    second = jnp.where(odd, cosine, sine)
    cos_out = jnp.where((turn == 1.0) | (turn == 2.0), -first, first)
    sin_out = jnp.where(turn >= 2.0, -second, second)
    return cos_out, sin_out


def tap_weights(coord):
    cell = jnp.floor(coord)
    ahead = coord - cell
    behind = 1.0 - ahead
    return cell, [
        behind * behind * behind * (1.0 / 6.0),
        2.0 / 3.0 + ahead * ahead * (0.5 * ahead - 1.0),
        2.0 / 3.0 + behind * behind * (0.5 * behind - 1.0),
        ahead * ahead * ahead * (1.0 / 6.0),
    ]


def all_bytes(ref, sem):
    pltpu.make_async_copy(ref, ref, sem).wait()


def slab_kernel(
    bins,
    slabs,
    data_hbm,
    route_hbm,
    spoke_hbm,
    segment_hbm,
    count_hbm,
    sens_hbm,
    image_hbm,
    weight_hbm,
    x_table_hbm,
    z_table_hbm,
    out_ref,
    data,
    route,
    spoke,
    segment,
    count,
    sens,
    image,
    weight,
    x_table,
    z_table,
    stacked,
    placed_rows,
    tiles,
    coords,
    tiles_in,
    coords_in,
    above,
    below,
    own_edge,
    samples,
    row_real,
    row_imag,
    across,
    kernel_x,
    weighted,
    products,
    sending,
    received,
    widened,
    total,
    fold,
    load_sems,
    own_sems,
    send_sems,
    recv_sems,
    tile_send_sems,
    tile_recv_sems,
    group_send_sems,
    group_recv_sems,
):
    slab = lax.axis_index("slab")
    me = lax.axis_index("bin")
    half_slabs = slabs // HALVES
    half = lax.div(slab, half_slabs)
    place = lax.rem(slab, half_slabs)
    opposite = lax.rem(slab + half_slabs, slabs)
    sources = HALVES * bins
    parts = HALVES * KP
    depth = KP * slabs
    rows = 2 * NXI // slabs
    wide = out_ref.shape[1]
    blocks = data.shape[0]

    barrier = pltpu.get_barrier_semaphore()
    route_peers = [(side, step) for side in (0, 1) for step in (4, 5, 3, 6, 7, 1, 2, 0)]
    route_peers.remove((0, 0))

    def route_peer(across_half, step):
        return {
            "bin": lax.rem(me + step, bins),
            "slab": opposite if across_half else slab,
        }

    half_order = [(dz, dy, dc) for dz in (0, 1) for dy in (2, 1, 3) for dc in (0, 1)]
    half_order += [(1, 0, 0), (1, 0, 1), (0, 0, 1)]

    def half_peer(dz, dy, dc):
        z, y, core = lax.div(place, 8), lax.rem(lax.div(place, 2), 4), lax.rem(place, 2)
        return 8 * lax.rem(z + dz, 2) + 2 * lax.rem(y + dy, 4) + lax.rem(core + dc, 2)

    for pair in route_peers:
        pl.semaphore_signal(barrier, inc=1, device_id=route_peer(*pair), device_id_type=MESH)
    for hop in half_order:
        pl.semaphore_signal(
            barrier,
            inc=1,
            device_id={"slab": half * half_slabs + half_peer(*hop)},
            device_id_type=MESH,
        )

    loads = [
        pltpu.make_async_copy(from_ref, to_ref, load_sems.at[at])
        for at, (from_ref, to_ref) in enumerate(
            [
                (route_hbm, route),
                (spoke_hbm, spoke),
                (segment_hbm, segment),
                (count_hbm, count),
                (data_hbm, data),
                (image_hbm, image),
                (weight_hbm, weight),
                (x_table_hbm.at[half], x_table),
                (z_table_hbm, z_table),
                (sens_hbm, sens),
            ]
        )
    ]
    for copy in loads:
        copy.start()
    for copy in loads[:4]:
        copy.wait()

    row = iota((blocks, LANES), 0)
    lane = iota((blocks, LANES), 1)
    lane_block = lane & (blocks - 1)

    def column(ref_row):
        spread = jnp.broadcast_to(ref_row.astype(F32), (blocks, blocks))
        eye = iota((blocks, blocks), 0) == iota((blocks, blocks), 1)
        return jnp.sum(jnp.where(eye, spread, 0.0), axis=1, keepdims=True)

    route_col = jnp.broadcast_to(column(route[...]), (blocks, LANES))
    route_row = jnp.sum(jnp.where(row == lane_block, route_col, 0.0), axis=0, keepdims=True)
    same = route_col == jnp.broadcast_to(route_row, (blocks, LANES))
    rank_row = jnp.sum(jnp.where(same & (row < lane_block), 1.0, 0.0), axis=0, keepdims=True)
    rank_col = jnp.sum(jnp.where(same & (lane < row), 1.0, 0.0), axis=1, keepdims=True)
    slot_row = route_row * CAPK + rank_row

    turn_row = (spoke[...] * GOLDEN_STEP) & (TURN_STEPS - 1)
    columns = [column(turn_row >> 8), column(turn_row & 255), column(segment[...]), column(count[...])]
    slot_hit = rank_col == (lane & (CAPK - 1)).astype(F32)
    picks = [jnp.where(slot_hit, value, 0.0) for value in columns]
    picks = jnp.concatenate(picks, axis=1).astype(BF16)
    picks = jnp.concatenate(
        [picks, jnp.zeros((LANES - blocks, len(columns) * LANES), BF16)], axis=0
    )
    coord_shape = (8 * bins, LANES)
    out_row = iota(coord_shape, 0)
    out_lane = iota(coord_shape, 1)
    part_row = out_row & 7
    is_x = part_row < KP
    partition = jnp.where(is_x, part_row, part_row - KP)
    row_route = jnp.where(part_row < 2 * KP, KP * (out_row >> 3) + partition, -1).astype(F32)
    chosen = (row_route == jnp.broadcast_to(route_row, coord_shape)) & (out_lane < blocks)
    spread = jnp.dot(jnp.where(chosen, 1.0, 0.0).astype(BF16), picks, preferred_element_type=F32)
    turns = (256.0 * spread[:, :LANES] + spread[:, LANES : 2 * LANES]) * (1.0 / TURN_STEPS)
    cosine, sine = turn_waves(turns)
    sample = (2 * ((out_lane & 63) >> 2) + (out_lane >> 6)).astype(F32)
    radial = (P_SIZE * spread[:, 2 * LANES : 3 * LANES] + sample - RO // 2 + 0.5) * ((NG - 8) / RO)
    coord_x = jnp.where(sample < spread[:, 3 * LANES :], NG / 2 + radial * cosine, FAR)
    coord_y = NG / 2 + radial * sine
    coords[...] = jnp.where(is_x, coord_x, coord_y)

    def coord_rows(index):
        return pl.ds(pl.multiple_of(index * 8, 8), 8)

    def tile_rows(index, many=1):
        return pl.ds(pl.multiple_of(index * PC, PC), many * PC)

    my_source = half * bins + me
    image_copy = pltpu.make_async_remote_copy(
        image,
        above,
        send_sems.at[1],
        recv_sems.at[1],
        {"bin": lax.rem(me + bins - 1, bins)},
        MESH,
    )
    edge_copy = pltpu.make_async_remote_copy(
        own_edge, below, send_sems.at[2], recv_sems.at[2], {"bin": lax.rem(me + 1, bins)}, MESH
    )
    is_first = me == 0
    is_last = me == bins - 1
    loads[4].wait()
    big = (bins * KP * 16, LANES)
    place_row = iota(big, 0)
    place_lane = iota(big, 1)
    wanted = (CAPK * (place_row >> 4) + (place_row & 3)).astype(F32)
    hit = (wanted == jnp.broadcast_to(slot_row, big)) & (((place_row >> 2) & 3) == (place_lane >> 5))
    one_hot = jnp.where(hit, 1.0, 0.0).astype(BF16)
    for quarter in range(4):
        for fourth in range(4):
            first = (4 * fourth + quarter) * LANES
            to_rows = slice(quarter * blocks, (quarter + 1) * blocks)
            stacked[to_rows, fourth * LANES : (fourth + 1) * LANES] = data[:, first : first + LANES]
    placed_rows[...] = jnp.dot(one_hot, stacked[...], preferred_element_type=F32)
    half_lane = iota((PC, LANES), 1) < 64

    def turn_pair(pair, carry):
        base = pl.multiple_of(pair * 32, 32)
        pieces = [
            placed_rows[pl.ds(base + 16 * one, 16), fourth * LANES : (fourth + 1) * LANES]
            for one in range(2)
            for fourth in range(4)
        ]
        turned = jnp.concatenate(pieces, axis=0).T
        low, high = turned[:PC], turned[PC:]
        at = pl.multiple_of(pair * 2 * PC, 2 * PC)
        tiles[pl.ds(at, PC), :] = jnp.where(half_lane, low, pltpu.roll(high, 64, 1)).astype(BF16)
        tiles[pl.ds(at + PC, PC), :] = jnp.where(half_lane, pltpu.roll(low, 64, 1), high).astype(BF16)
        return carry

    lax.fori_loop(0, bins * KP // 2, turn_pair, 0)

    loads[5].wait()
    pl.semaphore_wait(barrier, len(route_peers) + half_slabs - 1)

    @pl.when(jnp.logical_not(is_first))
    def _():
        image_copy.start()

    for pair in route_peers:
        peer = route_peer(*pair)
        pltpu.make_async_remote_copy(
            coords.at[coord_rows(peer["bin"])],
            coords_in.at[coord_rows(my_source)],
            send_sems.at[0],
            recv_sems.at[0],
            peer,
            MESH,
        ).start()
    own_coords = pltpu.make_async_copy(
        coords.at[coord_rows(me)], coords_in.at[coord_rows(my_source)], own_sems.at[0]
    )
    own_coords.start()
    own_tiles = []
    for part in range(KP):
        slot = part * sources + my_source
        for pair in route_peers:
            peer = route_peer(*pair)
            pltpu.make_async_remote_copy(
                tiles.at[tile_rows(peer["bin"] * KP + part)],
                tiles_in.at[tile_rows(slot)],
                tile_send_sems.at[part],
                tile_recv_sems.at[part],
                peer,
                MESH,
            ).start()
        copy = pltpu.make_async_copy(
            tiles.at[tile_rows(me * KP + part)], tiles_in.at[tile_rows(slot)], own_sems.at[1 + part]
        )
        copy.start()
        own_tiles.append(copy)

    fold_row = iota(fold.shape, 0)
    fold_lane = iota(fold.shape, 1)
    folds = ((fold_lane >> 4) == (fold_row >> 7)) & ((fold_lane & 15) == (fold_row & 15))
    fold[...] = jnp.where(folds, 1.0, 0.0).astype(BF16)

    own_coords.wait()
    others = pl.ds(0, (sources - 1) * 8)
    all_bytes(coords_in.at[others], recv_sems.at[0])
    loads[7].wait()
    y_offset = (iota((WY, LANES), 0) - WY // 2).astype(F32)
    taps = [turn_waves(y_offset * (m / NG)) for m in range(1, 4)]

    def prepare(step, carry):
        side = lax.div(step, KP)
        part = lax.rem(step, KP)

        def prepare_source(source, carry):
            base = pl.multiple_of((side * bins + source) * 8, 8)
            coord_x = coords_in[pl.ds(base + part, 1), :]
            coord_y = coords_in[pl.ds(base + KP + part, 1), :]
            cell, weights = tap_weights(coord_y)
            steps = y_offset * (cell - (1.0 + NG // 2))
            base_turns = steps * (1.0 / NG)
            base_cos, base_sin = turn_waves(base_turns - jnp.floor(base_turns))
            sum_cos = jnp.broadcast_to(weights[0], (WY, LANES))
            sum_sin = jnp.zeros((WY, LANES), F32)
            for tap_weight, (tap_cos, tap_sin) in zip(weights[1:], taps):
                sum_cos = sum_cos + tap_weight * tap_cos
                sum_sin = sum_sin + tap_weight * tap_sin
            at = pl.ds(pl.multiple_of((step * bins + source) * WY, WY), WY)
            row_real[at, :] = sum_cos * base_cos - sum_sin * base_sin
            row_imag[at, :] = sum_cos * base_sin + sum_sin * base_cos
            lanes = pl.ds(pl.multiple_of(source * LANES, LANES), LANES)
            cell, weights = tap_weights(coord_x)
            tile = (16, LANES)
            weights = [jnp.broadcast_to(tap, tile).astype(BF16) for tap in weights]
            for block in range(0, NG, LANES):
                start = jnp.clip(cell - (1.0 + block), -8.0, LANES + 8.0)
                away = (iota(tile, 0).astype(F32) - start).astype(BF16)
                for first in range(0, LANES, tile[0]):
                    value = jnp.zeros(tile, BF16)
                    for tap, tap_weight in enumerate(weights):
                        value = jnp.where(away == jnp.array(tap - first, BF16), tap_weight, value)
                    across[block + first : block + first + tile[0], lanes] = value
            return carry

        lax.fori_loop(0, bins, prepare_source, 0)
        kernel_x[step] = lax.dot_general(
            across[...], x_table[...], (((0,), (0,)), ((), ())), preferred_element_type=F32
        ).astype(BF16)
        return carry

    lax.fori_loop(0, parts, prepare, 0)

    loads[6].wait()

    @pl.when(jnp.logical_not(is_last))
    def _():
        image_copy.wait_recv()

    @pl.when(is_last)
    def _():
        above[...] = image[...]

    lane = iota((depth, wide), 1)
    upper_half = ((lane >> 4) & 1) == 1
    from_lane = iota((wide // 2, wide), 0)
    to_lane = iota((wide // 2, wide), 1)
    widen_weight = jnp.where(from_lane == ((to_lane >> 5) << 4) + (to_lane & 15), 1.0, 0.0)
    difference = above[...] - image[...]
    square = difference * difference
    other = jnp.where(upper_half, pltpu.roll(square, 16, 1), pltpu.roll(square, wide - 16, 1))
    magnitude = jnp.sqrt(square + other + SMOOTHING * SMOOTHING)
    wide_weight = jnp.dot(
        weight[...], widen_weight, preferred_element_type=F32, precision=lax.Precision.HIGHEST
    )
    own_edge[...] = wide_weight * difference / magnitude

    @pl.when(jnp.logical_not(is_last))
    def _():
        edge_copy.start()

    @pl.when(is_first)
    def _():
        below[...] = jnp.zeros_like(below)

    def own_copy(group):
        return pltpu.make_async_copy(
            sending.at[group, place], received.at[group, place], own_sems.at[1 + KP + group]
        )

    def take_tiles(part):
        own_tiles[part].wait()
        others = tile_rows(part * sources, sources - 1)
        all_bytes(tiles_in.at[others], tile_recv_sems.at[part])

        def widen_samples(source, carry):
            slot = part * sources + source
            samples[slot] = tiles_in[tile_rows(slot), :].astype(F32)
            return carry

        lax.fori_loop(0, sources, widen_samples, 0)

    count_x = NXI // HALVES
    group_rows = 2 * GC * WY

    def grid_part(part, groups):
        def one_side(side, carry):
            step = side * KP + part

            def weigh(source, carry):
                at = pl.ds(pl.multiple_of((step * bins + source) * WY, WY), WY)
                real, imag = row_real[at, :], row_imag[at, :]
                lanes = pl.ds(pl.multiple_of(source * LANES, LANES), LANES)
                for at_group, group in enumerate(groups):
                    for coil in range(GC):
                        row = group * GC + coil
                        data_real = samples[part * sources + side * bins + source, row : row + 1, :]
                        data_imag = samples[part * sources + side * bins + source, row + C : row + C + 1, :]
                        first = at_group * group_rows + coil * WY
                        weighted[first : first + WY, lanes] = (
                            real * data_real - imag * data_imag
                        ).astype(BF16)
                        first = first + GC * WY
                        weighted[first : first + WY, lanes] = (
                            real * data_imag + imag * data_real
                        ).astype(BF16)
                return carry

            lax.fori_loop(0, bins, weigh, 0)
            products[: len(groups) * group_rows, :] = jnp.dot(
                weighted[: len(groups) * group_rows, :],
                kernel_x[step],
                preferred_element_type=F32,
            )
            shape = (half_slabs, rows // 2, LANES)
            at = pl.ds(pl.multiple_of(step * rows, rows), rows)
            for at_group, group in enumerate(groups):
                first = at_group * group_rows
                above_rows = slice(first, first + group_rows // 2)
                below_rows = slice(first + group_rows // 2, first + group_rows)
                real = products[above_rows, :count_x] - products[below_rows, count_x:]
                imag = products[below_rows, :count_x] + products[above_rows, count_x:]
                spectra = jnp.concatenate([real.T.reshape(shape), imag.T.reshape(shape)], axis=1)
                sending[group, :, at, :] = spectra.astype(BF16)
            return carry

        lax.fori_loop(0, HALVES, one_side, 0)

    def send_group(group):
        for hop in half_order:
            peer = half_peer(*hop)
            pltpu.make_async_remote_copy(
                sending.at[group, peer],
                received.at[group, place],
                group_send_sems.at[group],
                group_recv_sems.at[group],
                {"slab": half * half_slabs + peer},
                MESH,
            ).start()
        own_copy(group).start()

    early = tuple(range(COIL_GROUPS // 2))
    late = tuple(range(COIL_GROUPS // 2, COIL_GROUPS))
    for part in range(KP - 1):
        take_tiles(part)
        grid_part(part, early)
    take_tiles(KP - 1)
    for group in early:
        grid_part(KP - 1, (group,))
        send_group(group)
    for group in late:
        for part in range(KP):
            grid_part(part, (group,))
        send_group(group)

    loads[8].wait()
    loads[9].wait()
    features = GC * WY
    for group in range(COIL_GROUPS):
        own_copy(group).wait()
        others = pl.ds(0, half_slabs - 1)
        all_bytes(received.at[group, others], group_recv_sems.at[group])

        def widen(source, carry, group=group):
            at = pl.ds(source * parts, parts)
            widened[at] = received[group, source].astype(F32).reshape(parts, rows, LANES)
            return carry

        lax.fori_loop(0, half_slabs, widen, 0)
        for pair in range(rows // 4):
            inputs = []
            for at_x in (2 * pair, 2 * pair + 1):
                real = widened[:, at_x, :].astype(BF16)
                imag = widened[:, rows // 2 + at_x, :].astype(BF16)
                inputs.append(jnp.concatenate([real, imag], axis=0))
            images = jnp.dot(
                z_table[...], jnp.concatenate(inputs, axis=1), preferred_element_type=F32
            )
            for at, at_x in enumerate((2 * pair, 2 * pair + 1)):
                image_real = images[:depth, at * LANES : (at + 1) * LANES]
                image_imag = images[depth:, at * LANES : (at + 1) * LANES]
                first = 2 * at_x * C * WY + group * features
                sens_real = sens[:, first : first + features].astype(F32)
                first = first + C * WY
                sens_imag = sens[:, first : first + features].astype(F32)
                real = sens_real * image_real + sens_imag * image_imag
                imag = sens_real * image_imag - sens_imag * image_real
                if group > 0:
                    real = real + total[2 * at_x]
                    imag = imag + total[2 * at_x + 1]
                total[2 * at_x] = real
                total[2 * at_x + 1] = imag

    others = pl.ds(0, half_slabs - 1)
    for group in range(COIL_GROUPS):
        all_bytes(sending.at[group, others], group_send_sems.at[group])
    all_bytes(coords_in.at[pl.ds(0, (sources - 1) * 8)], send_sems.at[0])
    for part in range(KP):
        all_bytes(tiles_in.at[tile_rows(0, sources - 1)], tile_send_sems.at[part])

    @pl.when(jnp.logical_not(is_first))
    def _():
        image_copy.wait_send()
        edge_copy.wait_recv()

    @pl.when(jnp.logical_not(is_last))
    def _():
        edge_copy.wait_send()

    scaling = 1.0 / math.sqrt(P_SIZE * bins * BLKB * depth * C / KP)
    for part in range(rows // 8):
        lanes = slice(part * LANES, (part + 1) * LANES)
        value = jnp.concatenate([total[part * 8 + at] for at in range(8)], axis=1)
        high = value.astype(BF16)
        low = (value - high.astype(F32)).astype(BF16)
        line = jnp.dot(high, fold[...], preferred_element_type=F32)
        line = line + jnp.dot(low, fold[...], preferred_element_type=F32)
        out_ref[:, lanes] = below[:, lanes] - own_edge[:, lanes] - line * scaling


def slab_gradient(
    bins, slabs, data, route, spoke, segment, count, sens, image, weight, x_table, z_table
):
    hbm = pl.BlockSpec(memory_space=pltpu.HBM)
    depth = sens.shape[0]
    blocks = data.shape[0]
    rows = 2 * NXI // slabs
    sources = HALVES * bins
    parts = HALVES * KP
    half_slabs = slabs // HALVES
    operands = (data, route, spoke, segment, count, sens, image, weight, x_table, z_table)
    held = operands[:8] + (x_table[0], z_table)
    return pl.pallas_call(
        functools.partial(slab_kernel, bins, slabs),
        out_shape=jax.ShapeDtypeStruct(image.shape, F32),
        in_specs=[hbm] * len(operands),
        out_specs=pl.BlockSpec(memory_space=pltpu.VMEM),
        scratch_shapes=[pltpu.VMEM(array.shape, array.dtype) for array in held]
        + [
            pltpu.VMEM((4 * blocks, 4 * LANES), BF16),
            pltpu.VMEM((bins * KP * 16, 4 * LANES), F32),
            pltpu.VMEM((bins * ROUTE_ROWS, LANES), BF16),
            pltpu.VMEM((bins * 8, LANES), F32),
            pltpu.VMEM((sources * ROUTE_ROWS, LANES), BF16),
            pltpu.VMEM((sources * 8, LANES), F32),
            pltpu.VMEM(image.shape, F32),
            pltpu.VMEM(image.shape, F32),
            pltpu.VMEM(image.shape, F32),
            pltpu.VMEM((KP * sources, PC, LANES), F32),
            pltpu.VMEM((parts * bins * WY, LANES), F32),
            pltpu.VMEM((parts * bins * WY, LANES), F32),
            pltpu.VMEM((NG, bins * LANES), BF16),
            pltpu.VMEM((parts, bins * LANES, 2 * NXI // HALVES), BF16),
            pltpu.VMEM((2 * C * WY, bins * LANES), BF16),
            pltpu.VMEM((2 * C * WY, 2 * NXI // HALVES), F32),
            pltpu.VMEM((COIL_GROUPS, half_slabs, parts * rows, LANES), BF16),
            pltpu.VMEM((COIL_GROUPS, half_slabs, parts * rows, LANES), BF16),
            pltpu.VMEM((depth, rows, LANES), F32),
            pltpu.VMEM((rows, depth, LANES), F32),
            pltpu.VMEM((8 * LANES, LANES), BF16),
            pltpu.SemaphoreType.DMA((len(operands),)),
            pltpu.SemaphoreType.DMA((1 + KP + COIL_GROUPS,)),
            pltpu.SemaphoreType.DMA((3,)),
            pltpu.SemaphoreType.DMA((3,)),
            pltpu.SemaphoreType.DMA((KP,)),
            pltpu.SemaphoreType.DMA((KP,)),
            pltpu.SemaphoreType.DMA((COIL_GROUPS,)),
            pltpu.SemaphoreType.DMA((COIL_GROUPS,)),
        ],
        compiler_params=pltpu.CompilerParams(
            collective_id=0, has_side_effects=True, vmem_limit_bytes=60 << 20
        ),
    )(*operands)


def waves(out_index, in_index, modulus):
    angles = 2.0 * math.pi / modulus * (out_index[:, None] * in_index[None, :] % modulus)
    return np.cos(angles), np.sin(angles)


def x_phases():
    cosine, sine = waves(np.arange(NXI) - NXI // 2, np.arange(NG) - NG // 2, NG)
    shape = (HALVES, NXI // HALVES, NG)
    table = np.concatenate([cosine.reshape(shape), sine.reshape(shape)], axis=1)
    return table.transpose(0, 2, 1)


def z_phases(slabs):
    depth = KP * slabs
    order = np.arange(depth).reshape(HALVES, slabs // HALVES, KP).transpose(1, 0, 2).reshape(-1)
    cosine, sine = waves(np.arange(depth) - depth // 2, order - depth // 2, depth)
    return np.concatenate(
        [np.concatenate([cosine, -sine], axis=1), np.concatenate([sine, cosine], axis=1)], axis=0
    )


def shards(
    sample_data,
    block_route,
    spoke_index,
    segment_index,
    sample_count,
    sensitivity,
    image,
    tv_weight,
):
    bins = lax.axis_size("bin")
    slabs = lax.axis_size("slab")
    gradient = slab_gradient(
        bins,
        slabs,
        sample_data,
        block_route.reshape(1, -1),
        spoke_index.reshape(1, -1),
        segment_index.reshape(1, -1),
        sample_count.reshape(1, -1),
        sensitivity,
        image[0],
        tv_weight[0],
        jnp.asarray(x_phases().astype(ml_dtypes.bfloat16)),
        jnp.asarray(z_phases(slabs).astype(ml_dtypes.bfloat16)),
    )
    return gradient.reshape(image.shape)


def solution(mesh):
    return jax.shard_map(
        shards,
        mesh=mesh,
        in_specs=(
            P(("bin", "slab"), None),
            P(("bin", "slab"), None),
            P(("bin", "slab")),
            P(("bin", "slab")),
            P(("bin", "slab")),
            P(None, "slab"),
            P("bin", None, "slab"),
            P("bin", None, "slab"),
        ),
        out_specs=P("bin", None, "slab"),
        check_vma=False,
    )
```
